128 devices in a mesh: group: 4 (over x_lo, core), tensor: 32 (over x_hi, y, z).
Axes of the slice: x: 4 (x_hi: 2, x_lo: 2; x = x_hi * 2 + x_lo), y: 4, z: 4, core: 2. Of those that a mesh axis runs over, the one named last changes fastest.
Arguments:
- tokens: bfloat16 [512, 3, 8192], P(('group', 'tensor')), may hold values from -6 to 6
- norm_gain: float32 [8192], replicated, may hold values from 0.25 to 1.75
- w_qkv: bfloat16 [8192, 10240], P(None, 'tensor'), may hold values from -0.0625 to 0.0625
- w_out: bfloat16 [8192, 8192], P('tensor'), may hold values from -0.0625 to 0.0625
- lengths: int32 [128, 4], P(('group', 'tensor')), may hold values from 1 to 512, 1024 in all within a row
- migrate: int32 [128, 4], P(('group', 'tensor')), may hold values from 0 to 3, as said below
- page_order: int32 [128, 12], P(('group', 'tensor')), may hold values from 0 to 11, each once within a row
- kv_pool: bfloat16 [128, 12, 2, 8, 128, 128], P(('group', 'tensor')), as said below
Outputs:
- mixed: bfloat16 [512, 3, 8192], P(('group', 'tensor'))
The draws below stay inside these ranges and needn't reach their ends.
Inputs may be any that keep to these rules, and one draw needn't show every extreme that they name: `migrate`: on each device every group number is named by exactly 1 row. The 4 lengths of one device sum to 1024. `kv_pool`: cached keys and values of order one or more.
All inputs are finite; a program needn't handle non-finite values.
Results may differ from the reference program's by a relative error of at most 0.013.
Values may be sent and summed in bfloat16 or wider, within the bound.
A program may use at most 128 MiB of HBM per device.

```python
import math
import jax
import jax.numpy as jnp
import numpy as np
from jax import lax

D = 8192
HEADS = 64
KV_HEADS = 8
HEAD_DIM = 128
PAGE = 128
MAX_PAGES = 4
STEPS = 3
ROW_DEV = 4
QKV = 10240
LEN_SUM = 1024
POOL = 12
DEVS = 128
ROWS_ALL = 512
N_GROUP = 4
N_TENSOR = 32


def draw_migrate(key, part):
    subkeys = jax.random.split(key, N_GROUP * N_TENSOR)

    def one_device(subkey):
        return jax.random.permutation(subkey, ROW_DEV)
    shuffled = jax.vmap(one_device)(subkeys)
    return (shuffled // (ROW_DEV // N_GROUP)).astype(jnp.int32)


def draw_kv_pool(key, part):
    shape = (N_GROUP * N_TENSOR, POOL, 2, KV_HEADS, PAGE, HEAD_DIM)
    return jax.random.normal(key, shape, jnp.float32).astype(jnp.bfloat16)


def block_levels(key, shape, pieces, smallest, high):
    level = 1.0
    for position, shards_of in pieces:
        steps = jax.random.uniform(jax.random.fold_in(jax.random.fold_in(key, 6), position), (shards_of,), jnp.float32, smallest / len(pieces), high / len(pieces))
        level = level * jnp.repeat(jnp.exp(steps), shape[position] // shards_of).reshape((-1,) + (1,) * (len(shape) - 1 - position))
    return level


def profile(number_of, total, reach, lean):
    portions = [(1 << 20) // math.isqrt(rank ** lean) + 1 for rank in range(2, number_of + 1)]
    surplus, given = total - reach - (number_of - 1), [1] * (number_of - 1)
    while surplus > 0:
        free = [i for i in range(number_of - 1) if given[i] < reach]
        pool, left = sum([portions[i] for i in free]), surplus
        for i in free:
            extra = min(reach - given[i], max(1, left * portions[i] // pool), surplus)
            given[i] = given[i] + extra
            surplus = surplus - extra
    return np.array([reach] + given)


def ragged_sizes(stream_key, count, total, most, lean):
    if count == 2:
        one = jax.random.randint(stream_key, (), max(1, total - most), min(most, total - 1) + 1)
        return jnp.stack([one, total - one])
    tallies = jnp.asarray(profile(count, total, most, lean), jnp.int32)
    couples = (count - 1) // 2
    donor, taker = tallies[1:1 + 2 * couples:2], tallies[2:2 + 2 * couples:2]
    room = jnp.minimum(donor - 1, most - taker)
    moved = jax.random.randint(jax.random.fold_in(stream_key, 1), (couples,), 0, 1 << 20) % (room + 1)
    tallies = tallies.at[1:1 + 2 * couples:2].set(donor - moved).at[2:2 + 2 * couples:2].set(taker + moved)
    return tallies[jax.random.permutation(jax.random.fold_in(stream_key, 2), count)]


def gaussian(key, shape, deviation, limit, cuts=(), kind=jnp.bfloat16):
    result = deviation * jax.random.normal(key, shape, jnp.float32)
    if cuts:
        result = result * block_levels(key, shape, cuts, -0.22, 0.18)
    return jnp.clip(result, -limit, limit).astype(kind)


def setup_inputs(seed: int = 0) -> dict:
    streams_of = jax.random.split(jax.random.key(seed), 9)
    tokens = gaussian(streams_of[0], (ROWS_ALL, STEPS, D), 1.0, 6.0, ((0, 128),))
    norm_gain = jnp.clip(1.0 + 0.15 * jax.random.normal(streams_of[1], (D,), jnp.float32), 0.25, 1.75)
    w_qkv = gaussian(streams_of[2], (D, QKV), D ** -0.5, 0.0625, ((1, 32),))
    w_out = gaussian(streams_of[3], (HEADS * HEAD_DIM, D), (HEADS * HEAD_DIM) ** -0.5, 0.0625, ((0, 32),))
    lengths = jax.vmap(lambda own: ragged_sizes(own, ROW_DEV, LEN_SUM, MAX_PAGES * PAGE, 2))(jax.random.split(streams_of[4], DEVS)).reshape((DEVS, ROW_DEV)).astype(jnp.int32)
    migrate = draw_migrate(jax.random.fold_in(streams_of[8], 71), 0)
    page_order = jax.vmap(lambda own: jax.random.permutation(own, POOL))(jax.random.split(streams_of[6], DEVS)).reshape((DEVS, POOL)).astype(jnp.int32)
    kv_pool = draw_kv_pool(jax.random.fold_in(streams_of[8], 71), 0)
    return {"tokens": tokens, "norm_gain": norm_gain, "w_qkv": w_qkv, "w_out": w_out, "lengths": lengths, "migrate": migrate, "page_order": page_order, "kv_pool": kv_pool}


EPS = 1e-05
ROPE_BASE = 500000.0
NEG_FILL = -1e+30

def rotate(values, positions):
    half_dim = values.shape[-1] // 2
    inverse = ROPE_BASE ** (-(jnp.arange(half_dim, dtype=jnp.float32) * 2.0 / values.shape[-1]))
    angles = positions.astype(jnp.float32)[..., None] * inverse
    cosine = jnp.cos(angles)[..., None, :]
    sine = jnp.sin(angles)[..., None, :]
    lower_half = values[..., :half_dim]
    upper_half = values[..., half_dim:]
    return jnp.concatenate([lower_half * cosine - upper_half * sine, upper_half * cosine + lower_half * sine], axis=-1)

def cache_stats(queries, pages, row_lens):
    row_total, steps_here, head_count, head_dim = queries.shape
    page_count = pages.shape[1]
    kv_heads = pages.shape[3]
    page_len = pages.shape[4]
    grouped = queries.reshape(row_total, steps_here, kv_heads, head_count // kv_heads, head_dim).astype(jnp.float32)
    scores = jnp.einsum('rskgd,rbktd->rskgbt', grouped, pages[:, :, 0].astype(jnp.float32)) * head_dim ** (-0.5)
    places = jnp.arange(page_count, dtype=jnp.int32)[:, None] * page_len + jnp.arange(page_len, dtype=jnp.int32)[None, :]
    inside = (places[None] < row_lens[:, None, None])[:, None, None, None]
    page_top = lax.optimization_barrier(jnp.max(jnp.where(inside, scores, NEG_FILL), axis=-1))
    weights = jnp.where(inside, jnp.exp(scores - page_top[..., None]), 0.0).astype(jnp.bfloat16)
    page_total = lax.optimization_barrier(jnp.sum(weights.astype(jnp.float32), axis=-1))
    page_acc = jnp.einsum('rskgbt,rbktd->rskgbd', weights.astype(jnp.float32), pages[:, :, 1].astype(jnp.float32))
    top_score = lax.optimization_barrier(jnp.max(page_top, axis=-1))
    page_scale = jnp.exp(page_top - top_score[..., None])
    return (top_score, lax.optimization_barrier(jnp.sum(page_scale * page_total, axis=-1)), lax.optimization_barrier(jnp.sum(page_scale[..., None] * page_acc, axis=-2)))

def finish(queries, cache_parts, all_keys, all_values, first_step):
    row_total, steps_here, head_count, head_dim = queries.shape
    kv_heads = all_keys.shape[2]
    grouped = queries.reshape(row_total, steps_here, kv_heads, head_count // kv_heads, head_dim).astype(jnp.float32)
    scores = jnp.einsum('rskgd,rukd->rskgu', grouped, all_keys.astype(jnp.float32)) * head_dim ** (-0.5)
    allowed = jnp.arange(all_keys.shape[1])[None, :] <= first_step + jnp.arange(steps_here)[:, None]
    allowed = allowed[None, :, None, None, :]
    new_top = lax.optimization_barrier(jnp.max(jnp.where(allowed, scores, NEG_FILL), axis=-1))
    weights = jnp.where(allowed, jnp.exp(scores - new_top[..., None]), 0.0).astype(jnp.bfloat16)
    new_total = lax.optimization_barrier(jnp.sum(weights.astype(jnp.float32), axis=-1))
    new_acc = jnp.einsum('rskgu,rukd->rskgd', weights.astype(jnp.float32), all_values.astype(jnp.float32))
    cache_top, cache_total, cache_acc = cache_parts
    top_score = jnp.maximum(cache_top, new_top)
    cache_scale = jnp.exp(cache_top - top_score)
    new_scale = jnp.exp(new_top - top_score)
    merged = (cache_scale[..., None] * cache_acc + new_scale[..., None] * new_acc) / (cache_scale * cache_total + new_scale * new_total)[..., None]
    return merged.reshape(row_total, steps_here, head_count * head_dim).astype(jnp.bfloat16)

def reference(tokens, norm_gain, w_qkv, w_out, lengths, migrate, page_order, kv_pool):
    devices = N_GROUP * N_TENSOR
    sendq = ROW_DEV // N_GROUP
    width_q = HEADS * HEAD_DIM
    width_k = KV_HEADS * HEAD_DIM
    slot_ids = jnp.arange(ROW_DEV, dtype=jnp.int32)
    order = jnp.argsort(migrate * ROW_DEV + slot_ids[None, :], axis=1).astype(jnp.int32)
    pages_used = (lengths + PAGE - 1) // PAGE
    offsets = (jnp.cumsum(pages_used, axis=1) - pages_used).astype(jnp.int32)
    group_ids = jnp.arange(N_GROUP, dtype=jnp.int32)[:, None, None]
    tensor_ids = jnp.arange(N_TENSOR, dtype=jnp.int32)[None, :, None]
    zero_block = jnp.zeros((N_GROUP, N_TENSOR, ROW_DEV), jnp.int32)
    old_device = ((slot_ids // sendq)[None, None, :] * N_TENSOR + tensor_ids + zero_block).reshape(devices, ROW_DEV)
    sorted_place = (group_ids * sendq + (slot_ids % sendq)[None, None, :] + zero_block).reshape(devices, ROW_DEV)
    old_slot = order[old_device, sorted_place]
    new_lengths = lengths[old_device, old_slot]
    first_page = offsets[old_device, old_slot]
    page_slots = jnp.clip(first_page[..., None] + jnp.arange(MAX_PAGES, dtype=jnp.int32), 0, POOL - 1).astype(jnp.int32)
    page_ids = page_order[old_device[..., None], page_slots]
    floats = tokens.astype(jnp.float32)
    normed = (floats * lax.rsqrt(lax.optimization_barrier(jnp.mean(floats * floats, axis=-1, keepdims=True)) + EPS) * norm_gain).astype(jnp.bfloat16)
    qkv = jnp.dot(normed.reshape(-1, D), w_qkv, preferred_element_type=jnp.float32).astype(jnp.bfloat16)
    qkv = qkv.reshape(ROWS_ALL, STEPS, QKV)
    positions = new_lengths.reshape(ROWS_ALL)[:, None] + jnp.arange(STEPS, dtype=jnp.int32)[None, :]
    queries = rotate(qkv[..., :width_q].reshape(ROWS_ALL, STEPS, HEADS, HEAD_DIM).astype(jnp.float32), positions).astype(jnp.bfloat16)
    new_keys = rotate(qkv[..., width_q:width_q + width_k].reshape(ROWS_ALL, STEPS, KV_HEADS, HEAD_DIM).astype(jnp.float32), positions).astype(jnp.bfloat16)
    new_values = qkv[..., width_q + width_k:].reshape(ROWS_ALL, STEPS, KV_HEADS, HEAD_DIM)

    def per_device(inputs):
        dev_queries, dev_keys, dev_values, dev_lens, dev_old, dev_pages = inputs
        pages = kv_pool[dev_old[:, None], dev_pages]
        parts = cache_stats(dev_queries, pages, dev_lens)
        return finish(dev_queries, parts, dev_keys, dev_values, 0)
    attended = lax.map(per_device, (queries.reshape(devices, ROW_DEV, STEPS, HEADS, HEAD_DIM), new_keys.reshape(devices, ROW_DEV, STEPS, KV_HEADS, HEAD_DIM), new_values.reshape(devices, ROW_DEV, STEPS, KV_HEADS, HEAD_DIM), new_lengths, old_device, page_ids))
    shard_cols = width_q // N_TENSOR
    attended = attended.reshape(ROWS_ALL * STEPS, N_TENSOR, shard_cols).transpose(1, 0, 2)
    weight_parts = w_out.reshape(N_TENSOR, shard_cols, D)

    def add_term(total, pair):
        term = jnp.dot(pair[0], pair[1], preferred_element_type=jnp.float32)
        return (total + lax.optimization_barrier(term.astype(jnp.bfloat16)).astype(jnp.float32), None)
    summed, unused = lax.scan(add_term, jnp.zeros((ROWS_ALL * STEPS, D), jnp.float32), (attended, weight_parts))
    return (floats + summed.reshape(ROWS_ALL, STEPS, D)).astype(jnp.bfloat16)
```

```python
import jax
import jax.numpy as jnp
import numpy as np
from jax import lax
from jax.experimental import pallas as pl
from jax.experimental.pallas import tpu as pltpu
from jax.sharding import PartitionSpec as P

MESH = pl.DeviceIdType.MESH
F32 = jnp.float32
BF16 = jnp.bfloat16
EPS = 1e-05
ROPE_BASE = 500000.0
NEG_FILL = -1e30
SCALE = 128 ** (-0.5)
D = 8192
MAIN = 6144
QW = 1536
CHUNK = 512
N_T = 32
N_G = 4


def body(
    tok, gain, inv, lens, mig, order, wqkv_hbm, wout_hbm, kv_hbm, out,
    stage, gsend, grecv, x32, xg, wq, wo, kv, qacc, qout, qin, heads, att, ain,
    terms, rq, rf, rx, fsend, frecv, o32,
    load_sem, gs_sem, gr_sem, s_sem, r_sem, as_sem, ar_sem,
):
    g = lax.axis_index("group")
    t = lax.axis_index("tensor")
    xh, y, z = t // 16, (t // 4) % 4, t % 4

    def idx(xx, yy, zz):
        return xx * 16 + lax.rem(yy + 4, 4) * 4 + lax.rem(zz + 4, 4)

    barrier = pltpu.get_barrier_semaphore()

    def greet(i, c):
        pl.semaphore_signal(
            barrier, inc=1, device_id=(g, lax.rem(t + i, N_T)), device_id_type=MESH
        )
        return c

    lax.fori_loop(1, N_T, greet, 0)
    for i in range(1, N_G):
        pl.semaphore_signal(
            barrier, inc=1, device_id=(lax.rem(g + i, N_G), t), device_id_type=MESH
        )

    loads = [
        pltpu.make_async_copy(wqkv_hbm, wq, load_sem.at[0]),
        pltpu.make_async_copy(kv_hbm, kv, load_sem.at[1]),
        pltpu.make_async_copy(wout_hbm, wo, load_sem.at[2]),
    ]
    for c in loads:
        c.start()

    for s in range(N_G):
        rows = tok[s].astype(F32)
        mean = jnp.mean(rows * rows, axis=-1, keepdims=True)
        normed = rows * lax.rsqrt(mean + EPS) * gain[...]
        for q in range(4):
            stage[s, 4 * q : 4 * q + 3, :] = normed[:, q * QW : (q + 1) * QW]
        for c in range(12):
            at = MAIN + (c % 4) * CHUNK
            lane = (c % 3) * CHUNK
            row = 4 * (c // 3) + 3
            stage[s, row : row + 1, lane : lane + CHUNK] = normed[
                c // 4 : c // 4 + 1, at : at + CHUNK
            ]
        gsend[s] = stage[s].astype(BF16)

    pl.semaphore_wait(barrier, N_T - 1 + N_G - 1)

    def group_exchange(src, dst, base):
        copies = []
        for i in range(1, N_G):
            to = lax.rem(g + i, N_G)
            copies.append(
                pltpu.make_async_remote_copy(
                    src_ref=src.at[to], dst_ref=dst.at[g],
                    send_sem=gs_sem.at[base + i], recv_sem=gr_sem.at[base + i],
                    device_id=(to, t), device_id_type=MESH,
                )
            )
            copies[-1].start()
        dst[g] = src[g]
        for c in copies:
            c.wait_recv()
        return copies

    sent = group_exchange(gsend, grecv, 0)
    for gg in range(N_G):
        stage[gg] = grecv[gg].astype(F32)
    for gg in range(N_G):
        for q in range(4):
            x32[q, 4 * gg : 4 * gg + 4, :] = stage[gg, 4 * q : 4 * q + 4, :]
    for q in range(4):
        xg[q, t] = x32[q].astype(BF16)

    def send(src, dst, k, to):
        c = pltpu.make_async_remote_copy(
            src_ref=src, dst_ref=dst, send_sem=s_sem.at[k], recv_sem=r_sem.at[k],
            device_id=(g, to), device_id_type=MESH,
        )
        c.start()
        sent.append(c)
        return c

    class Gather:
        def __init__(self, at, q, k):
            self.at, self.q, self.k, self.to = at[0], q, k, at[1]

        def start(self):
            ref = xg.at[pl.ds(self.q, 2), self.at(0)]
            self.up = send(ref, ref, self.k, self.to(1))
            self.down = send(ref, ref, self.k + 1, self.to(-1))

        def mid_up(self):
            self.up.wait_recv()
            ref = xg.at[self.q, self.at(-1)]
            self.up2 = send(ref, ref, self.k + 2, self.to(1))

        def mid_down(self):
            self.down.wait_recv()
            ref = xg.at[self.q + 1, self.at(1)]
            self.down2 = send(ref, ref, self.k + 3, self.to(-1))

        def mid(self):
            self.mid_up()
            self.mid_down()

        def end(self):
            self.up2.wait_recv()
            self.down2.wait_recv()

    def place(half, xx, first, second):
        return idx(xx, y + first, z + second) if half == 0 else idx(xx, y + second, z + first)

    def ring_first(half, xx):
        return (lambda o: place(half, xx, o, 0)), (lambda o: place(half, xh, o, 0))

    def ring_second(half, xx, e):
        return (lambda o: place(half, xx, e, o)), (lambda o: place(half, xh, 0, o))

    OFFS = (0, -1, 1, 2)
    own, peer = xh, 1 - xh

    class GatherSet:
        def __init__(self, xx, n):
            self.one = [Gather(ring_first(h, xx), 2 * h, 40 * n + 20 * h) for h in (0, 1)]
            self.two = [
                {
                    e: Gather(ring_second(h, xx, e), 2 * h, 40 * n + 20 * h + 4 + 4 * i)
                    for i, e in enumerate(OFFS)
                }
                for h in (0, 1)
            ]

        def s1(self):
            for h in (0, 1):
                self.one[h].start()
            for h in (0, 1):
                self.two[h][0].start()

        def s2(self):
            for h in (0, 1):
                self.one[h].mid_up()
                self.two[h][-1].start()
                self.one[h].mid_down()
                self.two[h][1].start()

        def mid(self, e):
            for h in (0, 1):
                self.two[h][e].mid()

        def s4(self):
            for h in (0, 1):
                self.one[h].end()
                self.two[h][2].start()

        def end(self, e):
            for h in (0, 1):
                self.two[h][e].end()

    far = idx(peer, y, z)
    row16 = lax.broadcasted_iota(jnp.int32, (256, 1), 0) & 3

    def project(xx):
        def lhs(q, a=0, b=QW):
            return xg[q, pl.ds(xx * 16, 16), :, a:b].reshape(256, b - a)

        def dot(l, a, b):
            return jnp.dot(l, wq[a:b, :], preferred_element_type=F32)

        m = MAIN
        main = dot(lhs(0), 0, QW)
        for q in (1, 2, 3):
            main = main + dot(lhs(q), q * QW, (q + 1) * QW)
        tails = (
            dot(lhs(0), m, m + 1536) + dot(lhs(1, 0, 512), m + 1536, m + 2048),
            dot(lhs(1, 512, 1536), m, m + 1024) + dot(lhs(2, 0, 1024), m + 1024, m + 2048),
            dot(lhs(2, 1024, 1536), m, m + 512) + dot(lhs(3), m + 512, m + 2048),
        )
        add = jnp.zeros_like(main)
        for s in range(3):
            qacc[:, 0:320] = tails[s]
            add = jnp.where(row16 == s, pltpu.roll(qacc[...], 256 - (3 - s), 0)[:, 0:320], add)
        qacc[:, 0:320] = jnp.where(row16 == 3, 0.0, main + add)
        qacc[:, 320:384] = jnp.zeros((256, 64), F32)
        flat = qacc[...]
        flat = jnp.where(lax.rem(t, 2) == 1, pltpu.roll(flat, 64, 1), flat)
        qout[pl.ds(xx * 16, 16)] = flat.reshape(16, 16, 384).astype(BF16)

    def a2a(src, dst, base, to):
        return pltpu.make_async_remote_copy(
            src_ref=src, dst_ref=dst.at[t],
            send_sem=as_sem.at[base + to], recv_sem=ar_sem.at[base + t],
            device_id=(g, to), device_id_type=MESH,
        )

    def a2a_wait(src, dst, base):
        def one(i, c):
            fr = lax.rem(t + i, N_T)
            d = pltpu.make_async_remote_copy(
                src_ref=src.at[fr], dst_ref=dst.at[fr],
                send_sem=as_sem.at[base + fr], recv_sem=ar_sem.at[base + fr],
                device_id=(g, fr), device_id_type=MESH,
            )
            d.wait_recv()
            d.wait_send()
            return c

        lax.fori_loop(1, N_T, one, 0)

    near_set, far_set = GatherSet(own, 0), GatherSet(peer, 1)
    near_set.s1()
    whole = xg.at[:, t]
    across = send(whole, whole, 160, far)
    near_set.s2()
    near_set.mid(0)
    near_set.s4()
    across.wait_recv()
    far_set.s1()
    near_set.mid(-1)
    near_set.mid(1)
    far_set.s2()
    near_set.mid(2)
    for e in OFFS:
        near_set.end(e)
    far_set.mid(0)
    far_set.s4()
    far_set.mid(-1)
    far_set.mid(1)
    loads[0].wait()
    project(own)

    def send_near(i, c):
        to = own * 16 + lax.rem(t + i, 16)
        a2a(qout.at[to], qin, 0, to).start()
        return c

    lax.fori_loop(1, 16, send_near, 0)
    qin[t] = qout[t]
    far_set.mid(2)
    for e in OFFS:
        far_set.end(e)
    project(peer)

    def send_far(i, c):
        to = peer * 16 + lax.rem(t + i, 16)
        a2a(qout.at[to], qin, 0, to).start()
        return c

    lax.fori_loop(0, 16, send_far, 0)

    used = [(lens[0, j] + 127) // 128 for j in range(4)]
    first = [0, used[0], used[0] + used[1], used[0] + used[1] + used[2]]

    def of_group(values, gg):
        total = jnp.int32(0)
        for j in range(4):
            total = total + jnp.where(mig[0, j] == gg, values[j], 0)
        return total

    row_len = [of_group([lens[0, j] for j in range(4)], gg) for gg in range(N_G)]
    pages = [
        [order[0, jnp.clip(of_group(first, gg) + b, 0, 11)] for b in range(4)]
        for gg in range(N_G)
    ]

    def by_row(rows, values):
        kind = (rows & 15) >> 2
        got = jnp.where(kind == 0, values[0], values[1])
        got = jnp.where(kind == 2, values[2], got)
        return jnp.where(kind == 3, values[3], got)

    r16 = lax.broadcasted_iota(jnp.int32, (16, 128), 0)
    angle = (by_row(r16, row_len) + (r16 & 3)).astype(F32) * inv[...]
    lane16 = lax.broadcasted_iota(jnp.int32, (16, 128), 1)
    cosine = jnp.cos(angle)
    sine = jnp.where(lane16 < 64, -jnp.sin(angle), jnp.sin(angle))

    a2a_wait(qout, qin, 0)

    def pair(p, c):
        even, odd = qin[2 * p].astype(F32), qin[2 * p + 1].astype(F32)
        five = (
            even[:, 0:128], even[:, 128:256],
            jnp.where(lane16 < 64, even[:, 256:384], odd[:, 0:128]),
            odd[:, 128:256], odd[:, 256:384],
        )
        for i, h in enumerate(five):
            turned = h * cosine + pltpu.roll(h, 64, 1) * sine
            heads[5 * p + i] = jnp.where(5 * p + i < 72, turned, h).astype(BF16)
        return c

    lax.fori_loop(0, 16, pair, 0)

    loads[1].wait()
    r128 = lax.broadcasted_iota(jnp.int32, (128, 128), 0)
    c128 = lax.broadcasted_iota(jnp.int32, (128, 128), 1)
    lim = by_row(r128, row_len)
    fresh = (
        (c128 < 16) & ((c128 >> 2) == ((r128 & 15) >> 2)) & ((c128 & 3) <= (r128 & 3))
    )
    pad = jnp.zeros((112, 128), BF16)

    def attend(k, c):
        queries = heads[pl.ds(8 * k, 8)].reshape(128, 128)

        def scores(keys):
            return lax.dot_general(
                queries, keys, (((1,), (1,)), ((), ())), preferred_element_type=F32
            )

        blocks, masks = [], []
        for b in range(4):
            blocks.append(
                by_row(r128, [scores(kv[pages[gg][b], 0, k]) for gg in range(N_G)]) * SCALE
            )
            masks.append(c128 + b * 128 < lim)
        blocks.append(scores(jnp.concatenate([heads[64 + k], pad], axis=0)) * SCALE)
        masks.append(fresh)
        tops = [jnp.where(m, s, NEG_FILL) for m, s in zip(masks, blocks)]
        top = tops[0]
        for s in tops[1:]:
            top = jnp.maximum(top, s)
        top = jnp.max(top, axis=-1, keepdims=True)
        weights = [
            jnp.where(m, jnp.exp(s - top), 0.0).astype(BF16) for m, s in zip(masks, tops)
        ]
        total = weights[0].astype(F32)
        for w in weights[1:]:
            total = total + w.astype(F32)
        total = jnp.sum(total, axis=-1, keepdims=True)
        acc = []
        for gg in range(N_G):
            a = jnp.dot(weights[0], kv[pages[gg][0], 1, k], preferred_element_type=F32)
            for b in (1, 2, 3):
                a = a + jnp.dot(
                    weights[b], kv[pages[gg][b], 1, k], preferred_element_type=F32
                )
            acc.append(a)
        acc = by_row(r128, acc) + jnp.dot(
            weights[4],
            jnp.concatenate([heads[72 + k], pad], axis=0),
            preferred_element_type=F32,
        )
        att[pl.ds(4 * k, 4)] = (acc / total).reshape(4, 2, 16, 128).astype(BF16)

        def give(i, c):
            to = 4 * k + i

            @pl.when(to != t)
            def _():
                a2a(att.at[to], ain, N_T, to).start()

            return c

        lax.fori_loop(0, 4, give, 0)
        return c

    lax.fori_loop(0, 8, attend, 0)
    ain[t] = att[t]
    loads[2].wait()
    a2a_wait(att, ain, N_T)

    def lhs_of(xx):
        left = jnp.concatenate(
            [ain[pl.ds(xx * 16, 16), i].reshape(256, 128) for i in (0, 1)], axis=1
        )
        wide = left.astype(F32)
        return left, [pltpu.roll(wide, 3 - s, 0).astype(BF16) for s in range(3)]

    def expand(sides, xx, half):
        left, turned = sides
        for c in range(6 * half, 6 * half + 6):
            at = MAIN + (c % 4) * CHUNK
            main = jnp.dot(
                left, wo[:, c * CHUNK : (c + 1) * CHUNK], preferred_element_type=F32
            )
            tail = jnp.dot(turned[c // 4], wo[:, at : at + CHUNK], preferred_element_type=F32)
            lane = (c % 3) * CHUNK
            terms[c // 3, pl.ds(xx * 16, 16), :, lane : lane + CHUNK] = (
                jnp.where(row16 == 3, tail, main).reshape(16, 16, CHUNK).astype(BF16)
            )

    class Reduce:
        def __init__(self, at, q, k, n):
            self.at, self.to = at
            self.q, self.k, self.n = q, k, n

        def s1(self):
            q, k, n = self.q, self.k, self.n
            self.up = send(terms.at[q, self.at(2)], rq.at[n, 0], k, self.to(1))
            self.down = send(terms.at[q + 1, self.at(-2)], rq.at[n, 1], k + 1, self.to(-1))

        def s2(self):
            q, k, n = self.q, self.k, self.n
            self.up.wait_recv()
            a = self.at(1)
            terms[q, a] = (terms[q, a].astype(F32) + rq[n, 0].astype(F32)).astype(BF16)
            self.up2 = send(terms.at[pl.ds(q, 2), a], rf.at[n, 0], k + 2, self.to(1))
            self.down.wait_recv()
            b = self.at(-1)
            terms[q + 1, b] = (terms[q + 1, b].astype(F32) + rq[n, 1].astype(F32)).astype(BF16)
            self.down2 = send(terms.at[pl.ds(q, 2), b], rf.at[n, 1], k + 3, self.to(-1))

        def s3(self):
            q, n = self.q, self.n
            self.up2.wait_recv()
            self.down2.wait_recv()
            a = self.at(0)
            for i in (0, 1):
                terms[q + i, a] = (
                    terms[q + i, a].astype(F32)
                    + rf[n, 0, i].astype(F32)
                    + rf[n, 1, i].astype(F32)
                ).astype(BF16)

    class ReduceSet:
        def __init__(self, xx, n):
            k, m = 161 + 40 * n, 10 * n
            self.big = [
                {
                    e: Reduce(
                        ring_second(h, xx, e), 2 * h, k + 20 * h + 4 * i, m + 5 * h + i
                    )
                    for i, e in enumerate(OFFS)
                }
                for h in (0, 1)
            ]
            self.last = [
                Reduce(ring_first(h, xx), 2 * h, k + 20 * h + 16, m + 5 * h + 4) for h in (0, 1)
            ]

        def s1(self, h):
            for e in (2, -1, 1, 0):
                self.big[h][e].s1()

        def s2(self, *es):
            for e in es:
                for h in (0, 1):
                    self.big[h][e].s2()

        def s3(self, *es):
            for e in es:
                for h in (0, 1):
                    self.big[h][e].s3()

        def l1(self):
            for h in (0, 1):
                self.last[h].s1()

        def l2(self):
            for h in (0, 1):
                self.last[h].s2()

        def l3(self):
            for h in (0, 1):
                self.last[h].s3()

    far_sum, near_sum = ReduceSet(peer, 0), ReduceSet(own, 1)
    sides = lhs_of(peer)
    expand(sides, peer, 0)
    far_sum.s1(0)
    expand(sides, peer, 1)
    far_sum.s1(1)
    far_sum.s2(2, -1, 1, 0)
    sides = lhs_of(own)
    expand(sides, own, 0)
    near_sum.s1(0)
    expand(sides, own, 1)
    near_sum.s1(1)
    far_sum.s3(2)
    far_sum.l1()
    near_sum.s2(2)
    far_sum.s3(-1, 1)
    far_sum.l2()
    near_sum.s2(-1, 1)
    far_sum.s3(0)
    far_sum.l3()
    over = send(terms.at[:, far], rx, 241, far)
    near_sum.s2(0)
    near_sum.s3(2)
    near_sum.l1()
    near_sum.s3(-1, 1)
    near_sum.l2()
    near_sum.s3(0)
    near_sum.l3()
    over.wait_recv()
    for q in range(4):
        x32[q] = terms[q, t].astype(F32) + rx[q].astype(F32)
    for gg in range(N_G):
        for q in range(4):
            stage[gg, 4 * q : 4 * q + 4, :] = x32[q, 4 * gg : 4 * gg + 4, :]
    for gg in range(N_G):
        fsend[gg] = stage[gg].astype(BF16)
    sent.extend(group_exchange(fsend, frecv, N_G))
    for s in range(N_G):
        stage[s] = frecv[s].astype(F32)
        for q in range(4):
            o32[s, :, q * QW : (q + 1) * QW] = stage[s, 4 * q : 4 * q + 3, :]
        for c in range(12):
            at = MAIN + (c % 4) * CHUNK
            lane = (c % 3) * CHUNK
            row = 4 * (c // 3) + 3
            o32[s, c // 4 : c // 4 + 1, at : at + CHUNK] = stage[
                s, row : row + 1, lane : lane + CHUNK
            ]
        out[s] = (tok[s].astype(F32) + o32[s]).astype(BF16)
    for c in sent:
        c.wait_send()


def per_device(tokens, norm_gain, w_qkv, w_out, lengths, migrate, page_order, kv_pool):
    half = np.arange(64, dtype=np.float32)
    inverse = jnp.float32(ROPE_BASE) ** (-(jnp.asarray(half) * 2.0 / 128))
    inverse = jnp.concatenate([inverse, inverse]).reshape(1, 128)
    vmem = pl.BlockSpec(memory_space=pltpu.VMEM)
    smem = pl.BlockSpec(memory_space=pltpu.SMEM)
    hbm = pl.BlockSpec(memory_space=pl.ANY)
    dma = pltpu.SemaphoreType.DMA
    return pl.pallas_call(
        body,
        out_shape=jax.ShapeDtypeStruct((4, 3, D), BF16),
        in_specs=[vmem, vmem, vmem, smem, smem, smem, hbm, hbm, hbm],
        out_specs=vmem,
        scratch_shapes=[
            pltpu.VMEM((4, 16, QW), F32),
            pltpu.VMEM((4, 16, QW), BF16),
            pltpu.VMEM((4, 16, QW), BF16),
            pltpu.VMEM((4, 16, QW), F32),
            pltpu.VMEM((4, 32, 16, QW), BF16),
            pltpu.VMEM((D, 320), BF16),
            pltpu.VMEM((256, D), BF16),
            pltpu.VMEM((12, 2, 8, 128, 128), BF16),
            pltpu.VMEM((256, 384), F32),
            pltpu.VMEM((32, 16, 384), BF16),
            pltpu.VMEM((32, 16, 384), BF16),
            pltpu.VMEM((80, 16, 128), BF16),
            pltpu.VMEM((32, 2, 16, 128), BF16),
            pltpu.VMEM((32, 2, 16, 128), BF16),
            pltpu.VMEM((4, 32, 16, QW), BF16),
            pltpu.VMEM((20, 2, 16, QW), BF16),
            pltpu.VMEM((20, 2, 2, 16, QW), BF16),
            pltpu.VMEM((4, 16, QW), BF16),
            pltpu.VMEM((4, 16, QW), BF16),
            pltpu.VMEM((4, 16, QW), BF16),
            pltpu.VMEM((4, 3, D), F32),
            dma((3,)),
            dma((2 * N_G,)),
            dma((2 * N_G,)),
            dma((242,)),
            dma((242,)),
            dma((2 * N_T,)),
            dma((2 * N_T,)),
        ],
        compiler_params=pltpu.CompilerParams(
            collective_id=0, has_side_effects=True, vmem_limit_bytes=60 * 2**20
        ),
        cost_estimate=pl.CostEstimate(
            flops=4 * 10**9, bytes_accessed=17 * 10**6, transcendentals=10**6
        ),
    )(
        tokens, norm_gain.reshape(1, D), inverse, lengths, migrate, page_order,
        w_qkv, w_out, kv_pool.reshape(12, 2, 8, 128, 128),
    )


def solution(mesh):
    both = ("group", "tensor")
    return jax.shard_map(
        per_device,
        mesh=mesh,
        in_specs=(
            P(both, None, None),
            P(),
            P(None, "tensor"),
            P("tensor", None),
            P(both, None),
            P(both, None),
            P(both, None),
            P(both, None, None, None, None, None),
        ),
        out_specs=P(both, None, None),
        check_vma=False,
    )
```

```python
import jax
import jax.numpy as jnp
import numpy as np
from jax import lax
from jax.experimental import pallas as pl
from jax.experimental.pallas import tpu as pltpu
from jax.sharding import PartitionSpec as P

MESH = pl.DeviceIdType.MESH
F32 = jnp.float32
BF16 = jnp.bfloat16
EPS = 1e-05
ROPE_BASE = 500000.0
NEG_FILL = -1e30
SCALE = 128 ** (-0.5)
D = 8192
MAIN = 6144
QW = 1536
CHUNK = 512
N_T = 32
N_G = 4


def body(
    tok, gain, inv, lens, mig, order, wqkv_hbm, wout_hbm, kv_hbm, out,
    stage, gsend, grecv, x32, xg, wq, wo, kv, qacc, qout, qin, heads, att, ain,
    terms, rq, rf, rx, fsend, frecv, o32,
    load_sem, gs_sem, gr_sem, s_sem, r_sem, as_sem, ar_sem,
):
    g = lax.axis_index("group")
    t = lax.axis_index("tensor")
    xh, y, z = t // 16, (t // 4) % 4, t % 4

    def idx(xx, yy, zz):
        return xx * 16 + lax.rem(yy + 4, 4) * 4 + lax.rem(zz + 4, 4)

    barrier = pltpu.get_barrier_semaphore()

    near = [(g, idx(1 - xh, y, z))]
    near += [(g, idx(xh, y + d, z)) for d in (1, -1)]
    near += [(g, idx(xh, y, z + d)) for d in (1, -1)]
    near += [(lax.rem(g + i, N_G), t) for i in range(1, N_G)]
    for to in near:
        pl.semaphore_signal(barrier, inc=1, device_id=to, device_id_type=MESH)

    loads = [
        pltpu.make_async_copy(wqkv_hbm, wq, load_sem.at[0]),
        pltpu.make_async_copy(kv_hbm, kv, load_sem.at[1]),
        pltpu.make_async_copy(wout_hbm, wo, load_sem.at[2]),
    ]
    for c in loads:
        c.start()

    for j in range(3):
        rows = tok[j].astype(F32)
        mean = jnp.mean(rows * rows, axis=-1, keepdims=True)
        normed = rows * lax.rsqrt(mean + EPS) * gain[...]
        for s in range(N_G):
            for q in range(4):
                stage[s, 4 * q + j : 4 * q + j + 1, :] = normed[
                    s : s + 1, q * QW : (q + 1) * QW
                ]
            for c in range(4 * j, 4 * j + 4):
                at = MAIN + (c % 4) * CHUNK
                lane = (c % 3) * CHUNK
                row = 4 * (c // 3) + 3
                stage[s, row : row + 1, lane : lane + CHUNK] = normed[
                    s : s + 1, at : at + CHUNK
                ]
    for s in range(N_G):
        gsend[s] = stage[s].astype(BF16)

    pl.semaphore_wait(barrier, len(near))

    def group_exchange(src, dst, base):
        copies = []
        for i in range(1, N_G):
            to = lax.rem(g + i, N_G)
            copies.append(
                pltpu.make_async_remote_copy(
                    src_ref=src.at[to], dst_ref=dst.at[g],
                    send_sem=gs_sem.at[base + i], recv_sem=gr_sem.at[base + i],
                    device_id=(to, t), device_id_type=MESH,
                )
            )
            copies[-1].start()
        dst[g] = src[g]
        for c in copies:
            c.wait_recv()
        return copies

    sent = group_exchange(gsend, grecv, 0)
    for gg in range(N_G):
        stage[gg] = grecv[gg].astype(F32)
    for gg in range(N_G):
        for q in range(4):
            x32[q, 4 * gg : 4 * gg + 4, :] = stage[gg, 4 * q : 4 * q + 4, :]
    for q in range(4):
        xg[q, t] = x32[q].astype(BF16)

    def send(src, dst, k, to):
        c = pltpu.make_async_remote_copy(
            src_ref=src, dst_ref=dst, send_sem=s_sem.at[k], recv_sem=r_sem.at[k],
            device_id=(g, to), device_id_type=MESH,
        )
        c.start()
        sent.append(c)
        return c

    class Gather:
        def __init__(self, at, q, k):
            self.at, self.q, self.k, self.to = at[0], q, k, at[1]

        def start(self):
            ref = xg.at[pl.ds(self.q, 2), self.at(0)]
            self.up = send(ref, ref, self.k, self.to(1))
            self.down = send(ref, ref, self.k + 1, self.to(-1))

        def mid_up(self):
            self.up.wait_recv()
            ref = xg.at[self.q, self.at(-1)]
            self.up2 = send(ref, ref, self.k + 2, self.to(1))

        def mid_down(self):
            self.down.wait_recv()
            ref = xg.at[self.q + 1, self.at(1)]
            self.down2 = send(ref, ref, self.k + 3, self.to(-1))

        def mid(self):
            self.mid_up()
            self.mid_down()

        def end(self):
            self.up2.wait_recv()
            self.down2.wait_recv()

    def place(half, xx, first, second):
        return idx(xx, y + first, z + second) if half == 0 else idx(xx, y + second, z + first)

    def ring_first(half, xx):
        return (lambda o: place(half, xx, o, 0)), (lambda o: place(half, xh, o, 0))

    def ring_second(half, xx, e):
        return (lambda o: place(half, xx, e, o)), (lambda o: place(half, xh, 0, o))

    OFFS = (0, -1, 1, 2)
    own, peer = xh, 1 - xh

    class GatherSet:
        def __init__(self, xx, n):
            self.one = [Gather(ring_first(h, xx), 2 * h, 40 * n + 20 * h) for h in (0, 1)]
            self.two = [
                {
                    e: Gather(ring_second(h, xx, e), 2 * h, 40 * n + 20 * h + 4 + 4 * i)
                    for i, e in enumerate(OFFS)
                }
                for h in (0, 1)
            ]

        def s1(self):
            for h in (0, 1):
                self.one[h].start()
            for h in (0, 1):
                self.two[h][0].start()

        def s2(self):
            for h in (0, 1):
                self.one[h].mid_up()
                self.two[h][-1].start()
                self.one[h].mid_down()
                self.two[h][1].start()

        def mid(self, e):
            for h in (0, 1):
                self.two[h][e].mid()

        def s4(self):
            for h in (0, 1):
                self.one[h].end()
                self.two[h][2].start()

        def end(self, e):
            for h in (0, 1):
                self.two[h][e].end()

    far = idx(peer, y, z)
    row16 = lax.broadcasted_iota(jnp.int32, (256, 1), 0) & 3

    def project(xx):
        def lhs(q, a=0, b=QW):
            return xg[q, pl.ds(xx * 16, 16), :, a:b].reshape(256, b - a)

        def dot(l, a, b):
            return lax.dot_general(
                l, wq[:, a:b], (((1,), (1,)), ((), ())), preferred_element_type=F32
            )

        m = MAIN
        main = dot(lhs(0), 0, QW)
        for q in (1, 2, 3):
            main = main + dot(lhs(q), q * QW, (q + 1) * QW)
        tails = (
            dot(lhs(0), m, m + 1536) + dot(lhs(1, 0, 512), m + 1536, m + 2048),
            dot(lhs(1, 512, 1536), m, m + 1024) + dot(lhs(2, 0, 1024), m + 1024, m + 2048),
            dot(lhs(2, 1024, 1536), m, m + 512) + dot(lhs(3), m + 512, m + 2048),
        )
        add = jnp.zeros_like(main)
        for s in range(3):
            qacc[:, 0:320] = tails[s]
            add = jnp.where(row16 == s, pltpu.roll(qacc[...], 256 - (3 - s), 0)[:, 0:320], add)
        qacc[:, 0:320] = jnp.where(row16 == 3, 0.0, main + add)
        qacc[:, 320:384] = jnp.zeros((256, 64), F32)
        flat = qacc[...]
        flat = jnp.where(lax.rem(t, 2) == 1, pltpu.roll(flat, 64, 1), flat)
        qout[pl.ds(xx * 16, 16)] = flat.reshape(16, 16, 384).astype(BF16)

    def a2a(src, dst, base, to):
        return pltpu.make_async_remote_copy(
            src_ref=src, dst_ref=dst.at[t],
            send_sem=as_sem.at[base + to], recv_sem=ar_sem.at[base + t],
            device_id=(g, to), device_id_type=MESH,
        )

    def a2a_wait(src, dst, base):
        def one(i, c):
            fr = lax.rem(t + i, N_T)
            d = pltpu.make_async_remote_copy(
                src_ref=src.at[fr], dst_ref=dst.at[fr],
                send_sem=as_sem.at[base + fr], recv_sem=ar_sem.at[base + fr],
                device_id=(g, fr), device_id_type=MESH,
            )
            d.wait_recv()
            d.wait_send()
            return c

        lax.fori_loop(1, N_T, one, 0)

    near_set, far_set = GatherSet(own, 0), GatherSet(peer, 1)
    near_set.s1()
    whole = xg.at[:, t]
    across = send(whole, whole, 160, far)
    near_set.s2()
    near_set.mid(0)
    near_set.s4()
    across.wait_recv()
    far_set.s1()
    near_set.mid(-1)
    near_set.mid(1)
    far_set.s2()
    near_set.mid(2)
    for e in OFFS:
        near_set.end(e)
    far_set.mid(0)
    far_set.s4()
    far_set.mid(-1)
    far_set.mid(1)
    loads[0].wait()
    project(own)

    def send_near(i, c):
        to = own * 16 + lax.rem(t + i, 16)
        a2a(qout.at[to], qin, 0, to).start()
        return c

    lax.fori_loop(1, 16, send_near, 0)
    qin[t] = qout[t]
    far_set.mid(2)
    for e in OFFS:
        far_set.end(e)
    project(peer)

    def send_far(i, c):
        to = peer * 16 + lax.rem(t + i, 16)
        a2a(qout.at[to], qin, 0, to).start()
        return c

    lax.fori_loop(0, 16, send_far, 0)

    used = [(lens[0, j] + 127) // 128 for j in range(4)]
    first = [0, used[0], used[0] + used[1], used[0] + used[1] + used[2]]

    def of_group(values, gg):
        total = jnp.int32(0)
        for j in range(4):
            total = total + jnp.where(mig[0, j] == gg, values[j], 0)
        return total

    row_len = [of_group([lens[0, j] for j in range(4)], gg) for gg in range(N_G)]
    pages = [
        [order[0, jnp.clip(of_group(first, gg) + b, 0, 11)] for b in range(4)]
        for gg in range(N_G)
    ]

    def by_row(rows, values):
        kind = (rows & 15) >> 2
        got = jnp.where(kind == 0, values[0], values[1])
        got = jnp.where(kind == 2, values[2], got)
        return jnp.where(kind == 3, values[3], got)

    r16 = lax.broadcasted_iota(jnp.int32, (16, 128), 0)
    angle = (by_row(r16, row_len) + (r16 & 3)).astype(F32) * inv[...]
    lane16 = lax.broadcasted_iota(jnp.int32, (16, 128), 1)
    cosine = jnp.cos(angle)
    sine = jnp.where(lane16 < 64, -jnp.sin(angle), jnp.sin(angle))

    a2a_wait(qout, qin, 0)

    def pair(p, c):
        even, odd = qin[2 * p].astype(F32), qin[2 * p + 1].astype(F32)
        five = (
            even[:, 0:128], even[:, 128:256],
            jnp.where(lane16 < 64, even[:, 256:384], odd[:, 0:128]),
            odd[:, 128:256], odd[:, 256:384],
        )
        for i, h in enumerate(five):
            turned = h * cosine + pltpu.roll(h, 64, 1) * sine
            heads[5 * p + i] = jnp.where(5 * p + i < 72, turned, h).astype(BF16)
        return c

    lax.fori_loop(0, 16, pair, 0)

    loads[1].wait()
    r128 = lax.broadcasted_iota(jnp.int32, (128, 128), 0)
    c128 = lax.broadcasted_iota(jnp.int32, (128, 128), 1)
    lim = by_row(r128, row_len)
    fresh = (
        (c128 < 16) & ((c128 >> 2) == ((r128 & 15) >> 2)) & ((c128 & 3) <= (r128 & 3))
    )
    pad = jnp.zeros((112, 128), BF16)

    def attend(k, c):
        queries = heads[pl.ds(8 * k, 8)].reshape(128, 128)

        def scores(keys):
            return lax.dot_general(
                queries, keys, (((1,), (1,)), ((), ())), preferred_element_type=F32
            )

        blocks, masks = [], []
        for b in range(4):
            blocks.append(
                by_row(r128, [scores(kv[pages[gg][b], 0, k]) for gg in range(N_G)]) * SCALE
            )
            masks.append(c128 + b * 128 < lim)
        blocks.append(scores(jnp.concatenate([heads[64 + k], pad], axis=0)) * SCALE)
        masks.append(fresh)
        tops = [jnp.where(m, s, NEG_FILL) for m, s in zip(masks, blocks)]
        top = tops[0]
        for s in tops[1:]:
            top = jnp.maximum(top, s)
        top = jnp.max(top, axis=-1, keepdims=True)
        weights = [
            jnp.where(m, jnp.exp(s - top), 0.0).astype(BF16) for m, s in zip(masks, tops)
        ]
        total = weights[0].astype(F32)
        for w in weights[1:]:
            total = total + w.astype(F32)
        total = jnp.sum(total, axis=-1, keepdims=True)
        acc = []
        for gg in range(N_G):
            a = jnp.dot(weights[0], kv[pages[gg][0], 1, k], preferred_element_type=F32)
            for b in (1, 2, 3):
                a = a + jnp.dot(
                    weights[b], kv[pages[gg][b], 1, k], preferred_element_type=F32
                )
            acc.append(a)
        acc = by_row(r128, acc) + jnp.dot(
            weights[4],
            jnp.concatenate([heads[72 + k], pad], axis=0),
            preferred_element_type=F32,
        )
        att[pl.ds(4 * k, 4)] = (acc / total).reshape(4, 2, 16, 128).astype(BF16)

        def give(i, c):
            to = 4 * k + i

            @pl.when(to != t)
            def _():
                a2a(att.at[to], ain, N_T, to).start()

            return c

        lax.fori_loop(0, 4, give, 0)
        return c

    lax.fori_loop(0, 8, attend, 0)
    ain[t] = att[t]
    loads[2].wait()
    a2a_wait(att, ain, N_T)

    def lhs_of(xx):
        left = jnp.concatenate(
            [ain[pl.ds(xx * 16, 16), i].reshape(256, 128) for i in (0, 1)], axis=1
        )
        wide = left.astype(F32)
        return left, [pltpu.roll(wide, 3 - s, 0).astype(BF16) for s in range(3)]

    def expand(sides, xx, half):
        left, turned = sides
        for c in range(6 * half, 6 * half + 6):
            at = MAIN + (c % 4) * CHUNK
            main = jnp.dot(
                left, wo[:, c * CHUNK : (c + 1) * CHUNK], preferred_element_type=F32
            )
            tail = jnp.dot(turned[c // 4], wo[:, at : at + CHUNK], preferred_element_type=F32)
            lane = (c % 3) * CHUNK
            terms[c // 3, pl.ds(xx * 16, 16), :, lane : lane + CHUNK] = (
                jnp.where(row16 == 3, tail, main).reshape(16, 16, CHUNK).astype(BF16)
            )

    class Reduce:
        def __init__(self, at, q, k, n):
            self.at, self.to = at
            self.q, self.k, self.n = q, k, n

        def s1(self):
            q, k, n = self.q, self.k, self.n
            self.up = send(terms.at[q, self.at(2)], rq.at[n, 0], k, self.to(1))
            self.down = send(terms.at[q + 1, self.at(-2)], rq.at[n, 1], k + 1, self.to(-1))

        def s2(self):
            q, k, n = self.q, self.k, self.n
            self.up.wait_recv()
            a = self.at(1)
            terms[q, a] = (terms[q, a].astype(F32) + rq[n, 0].astype(F32)).astype(BF16)
            self.up2 = send(terms.at[pl.ds(q, 2), a], rf.at[n, 0], k + 2, self.to(1))
            self.down.wait_recv()
            b = self.at(-1)
            terms[q + 1, b] = (terms[q + 1, b].astype(F32) + rq[n, 1].astype(F32)).astype(BF16)
            self.down2 = send(terms.at[pl.ds(q, 2), b], rf.at[n, 1], k + 3, self.to(-1))

        def s3(self):
            q, n = self.q, self.n
            self.up2.wait_recv()
            self.down2.wait_recv()
            a = self.at(0)
            for i in (0, 1):
                terms[q + i, a] = (
                    terms[q + i, a].astype(F32)
                    + rf[n, 0, i].astype(F32)
                    + rf[n, 1, i].astype(F32)
                ).astype(BF16)

    class ReduceSet:
        def __init__(self, xx, n):
            k, m = 161 + 40 * n, 10 * n
            self.big = [
                {
                    e: Reduce(
                        ring_second(h, xx, e), 2 * h, k + 20 * h + 4 * i, m + 5 * h + i
                    )
                    for i, e in enumerate(OFFS)
                }
                for h in (0, 1)
            ]
            self.last = [
                Reduce(ring_first(h, xx), 2 * h, k + 20 * h + 16, m + 5 * h + 4) for h in (0, 1)
            ]

        def s1(self, h):
            for e in (2, -1, 1, 0):
                self.big[h][e].s1()

        def s2(self, *es):
            for e in es:
                for h in (0, 1):
                    self.big[h][e].s2()

        def s3(self, *es):
            for e in es:
                for h in (0, 1):
                    self.big[h][e].s3()

        def l1(self):
            for h in (0, 1):
                self.last[h].s1()

        def l2(self):
            for h in (0, 1):
                self.last[h].s2()

        def l3(self):
            for h in (0, 1):
                self.last[h].s3()

    far_sum, near_sum = ReduceSet(peer, 0), ReduceSet(own, 1)
    sides = lhs_of(peer)
    expand(sides, peer, 0)
    far_sum.s1(0)
    expand(sides, peer, 1)
    far_sum.s1(1)
    far_sum.s2(2, -1, 1, 0)
    sides = lhs_of(own)
    expand(sides, own, 0)
    near_sum.s1(0)
    expand(sides, own, 1)
    near_sum.s1(1)
    far_sum.s3(2)
    far_sum.l1()
    near_sum.s2(2)
    far_sum.s3(-1, 1)
    far_sum.l2()
    near_sum.s2(-1, 1)
    far_sum.s3(0)
    far_sum.l3()
    over = send(terms.at[:, far], rx, 241, far)
    near_sum.s2(0)
    near_sum.s3(2)
    near_sum.l1()
    near_sum.s3(-1, 1)
    near_sum.l2()
    near_sum.s3(0)
    near_sum.l3()
    over.wait_recv()
    for q in range(4):
        x32[q] = terms[q, t].astype(F32) + rx[q].astype(F32)
    for gg in range(N_G):
        for q in range(4):
            stage[gg, 4 * q : 4 * q + 4, :] = x32[q, 4 * gg : 4 * gg + 4, :]
    for gg in range(N_G):
        fsend[gg] = stage[gg].astype(BF16)
    sent.extend(group_exchange(fsend, frecv, N_G))
    for s in range(N_G):
        stage[s] = frecv[s].astype(F32)
        for j in range(3):
            for q in range(4):
                o32[j, s : s + 1, q * QW : (q + 1) * QW] = stage[
                    s, 4 * q + j : 4 * q + j + 1, :
                ]
            for c in range(4 * j, 4 * j + 4):
                at = MAIN + (c % 4) * CHUNK
                lane = (c % 3) * CHUNK
                row = 4 * (c // 3) + 3
                o32[j, s : s + 1, at : at + CHUNK] = stage[
                    s, row : row + 1, lane : lane + CHUNK
                ]
    for j in range(3):
        out[j] = (tok[j].astype(F32) + o32[j]).astype(BF16)
    for c in sent:
        c.wait_send()


def per_device(tokens, norm_gain, w_qkv, w_out, lengths, migrate, page_order, kv_pool):
    half = np.arange(64, dtype=np.float32)
    inverse = jnp.float32(ROPE_BASE) ** (-(jnp.asarray(half) * 2.0 / 128))
    inverse = jnp.concatenate([inverse, inverse]).reshape(1, 128)
    vmem = pl.BlockSpec(memory_space=pltpu.VMEM)
    smem = pl.BlockSpec(memory_space=pltpu.SMEM)
    hbm = pl.BlockSpec(memory_space=pl.ANY)
    dma = pltpu.SemaphoreType.DMA
    done = pl.pallas_call(
        body,
        out_shape=jax.ShapeDtypeStruct((3, 4, D), BF16),
        in_specs=[vmem, vmem, vmem, smem, smem, smem, hbm, hbm, hbm],
        out_specs=vmem,
        scratch_shapes=[
            pltpu.VMEM((4, 16, QW), F32),
            pltpu.VMEM((4, 16, QW), BF16),
            pltpu.VMEM((4, 16, QW), BF16),
            pltpu.VMEM((4, 16, QW), F32),
            pltpu.VMEM((4, 32, 16, QW), BF16),
            pltpu.VMEM((320, D), BF16),
            pltpu.VMEM((256, D), BF16),
            pltpu.VMEM((12, 2, 8, 128, 128), BF16),
            pltpu.VMEM((256, 384), F32),
            pltpu.VMEM((32, 16, 384), BF16),
            pltpu.VMEM((32, 16, 384), BF16),
            pltpu.VMEM((80, 16, 128), BF16),
            pltpu.VMEM((32, 2, 16, 128), BF16),
            pltpu.VMEM((32, 2, 16, 128), BF16),
            pltpu.VMEM((4, 32, 16, QW), BF16),
            pltpu.VMEM((20, 2, 16, QW), BF16),
            pltpu.VMEM((20, 2, 2, 16, QW), BF16),
            pltpu.VMEM((4, 16, QW), BF16),
            pltpu.VMEM((4, 16, QW), BF16),
            pltpu.VMEM((4, 16, QW), BF16),
            pltpu.VMEM((3, 4, D), F32),
            dma((3,)),
            dma((2 * N_G,)),
            dma((2 * N_G,)),
            dma((242,)),
            dma((242,)),
            dma((2 * N_T,)),
            dma((2 * N_T,)),
        ],
        compiler_params=pltpu.CompilerParams(
            collective_id=0, has_side_effects=True, vmem_limit_bytes=60 * 2**20
        ),
        cost_estimate=pl.CostEstimate(
            flops=4 * 10**9, bytes_accessed=17 * 10**6, transcendentals=10**6
        ),
    )(
        tokens.transpose(1, 0, 2), norm_gain.reshape(1, D), inverse, lengths, migrate, page_order,
        w_qkv.T, w_out, kv_pool.reshape(12, 2, 8, 128, 128),
    )
    return done.transpose(1, 0, 2)


def solution(mesh):
    both = ("group", "tensor")
    return jax.shard_map(
        per_device,
        mesh=mesh,
        in_specs=(
            P(both, None, None),
            P(),
            P(None, "tensor"),
            P("tensor", None),
            P(both, None),
            P(both, None),
            P(both, None),
            P(both, None, None, None, None, None),
        ),
        out_specs=P(both, None, None),
        check_vma=False,
    )
```

```python
import jax
import jax.numpy as jnp
import numpy as np
from jax import lax
from jax.experimental import pallas as pl
from jax.experimental.pallas import tpu as pltpu
from jax.sharding import PartitionSpec as P

MESH = pl.DeviceIdType.MESH
F32 = jnp.float32
BF16 = jnp.bfloat16
EPS = 1e-05
ROPE_BASE = 500000.0
NEG_FILL = -1e30
SCALE = 128 ** (-0.5)
D = 8192
MAIN = 6144
QW = 1536
CHUNK = 512
LX = 256
N_T = 32
N_G = 4


def body(
    gain, inv, lens, mig, order, tok_hbm, wqkv_hbm, wout_hbm, kv_hbm, out,
    tok, stage, gsend, grecv, x32, xg, wq, wo, kv, qacc, qout, qin, heads, att, ain,
    terms, rq, rf, rx, rc, fsend, frecv, o32,
    load_sem, gs_sem, gr_sem, s_sem, r_sem, as_sem, ar_sem,
):
    g = lax.axis_index("group")
    t = lax.axis_index("tensor")
    xh, y, z = t // 16, (t // 4) % 4, t % 4

    def idx(xx, yy, zz):
        return xx * 16 + lax.rem(yy + 4, 4) * 4 + lax.rem(zz + 4, 4)

    def spot(xx, yy, zz):
        return xx, lax.rem(yy + 4, 4), lax.rem(zz + 4, 4)

    barrier = pltpu.get_barrier_semaphore()
    first_load = pltpu.make_async_copy(tok_hbm, tok, load_sem.at[3])
    first_load.start()

    near = [(g, idx(1 - xh, y, z))]
    near += [(g, idx(xh, y + d, z)) for d in (1, -1)]
    near += [(g, idx(xh, y, z + d)) for d in (1, -1)]
    near += [(lax.rem(g + i, N_G), t) for i in range(1, N_G)]
    for to in near:
        pl.semaphore_signal(barrier, inc=1, device_id=to, device_id_type=MESH)

    loads = [
        pltpu.make_async_copy(wqkv_hbm, wq, load_sem.at[0]),
        pltpu.make_async_copy(kv_hbm, kv, load_sem.at[1]),
        pltpu.make_async_copy(wout_hbm, wo, load_sem.at[2]),
    ]
    for c in loads:
        c.start()

    first_load.wait()
    for j in range(3):
        rows = tok[j].astype(F32)
        mean = jnp.mean(rows * rows, axis=-1, keepdims=True)
        normed = rows * lax.rsqrt(mean + EPS) * gain[...]
        for s in range(N_G):
            for q in range(4):
                stage[s, 4 * q + j : 4 * q + j + 1, :] = normed[
                    s : s + 1, q * QW : (q + 1) * QW
                ]
            for c in range(4 * j, 4 * j + 4):
                at = MAIN + (c % 4) * CHUNK
                lane = (c % 3) * CHUNK
                row = 4 * (c // 3) + 3
                stage[s, row : row + 1, lane : lane + CHUNK] = normed[
                    s : s + 1, at : at + CHUNK
                ]
    for s in range(N_G):
        gsend[s] = stage[s].astype(BF16)

    pl.semaphore_wait(barrier, len(near))

    def group_exchange(src, dst, base):
        copies = []
        for i in range(1, N_G):
            to = lax.rem(g + i, N_G)
            copies.append(
                pltpu.make_async_remote_copy(
                    src_ref=src.at[to], dst_ref=dst.at[g],
                    send_sem=gs_sem.at[base + i], recv_sem=gr_sem.at[base + i],
                    device_id=(to, t), device_id_type=MESH,
                )
            )
            copies[-1].start()
        dst[g] = src[g]
        for c in copies:
            c.wait_recv()
        return copies

    sent = group_exchange(gsend, grecv, 0)
    for gg in range(N_G):
        stage[gg] = grecv[gg].astype(F32)
    for gg in range(N_G):
        for q in range(4):
            x32[q, 4 * gg : 4 * gg + 4, :] = stage[gg, 4 * q : 4 * q + 4, :]
    for q in range(4):
        xg[q, xh, y, z] = x32[q].astype(BF16)

    def send(src, dst, k, to):
        c = pltpu.make_async_remote_copy(
            src_ref=src, dst_ref=dst, send_sem=s_sem.at[k], recv_sem=r_sem.at[k],
            device_id=(g, to), device_id_type=MESH,
        )
        c.start()
        sent.append(c)
        return c

    class Gather:
        def __init__(self, at, q, k, lanes):
            (self.at, self.to), self.q, self.k = at, q, k
            self.lanes = slice(0, lanes)

        def block(self, o, one=None):
            if one is None:
                return xg.at[(pl.ds(self.q, 2), *self.at(o), slice(None), self.lanes)]
            return xg.at[(self.q + one, *self.at(o), slice(None), self.lanes)]

        def start(self):
            ref = self.block(0)
            self.up = send(ref, ref, self.k, self.to(1))
            self.down = send(ref, ref, self.k + 1, self.to(-1))

        def mid_up(self):
            self.up.wait_recv()
            ref = self.block(-1, 0)
            self.up2 = send(ref, ref, self.k + 2, self.to(1))

        def mid_down(self):
            self.down.wait_recv()
            ref = self.block(1, 1)
            self.down2 = send(ref, ref, self.k + 3, self.to(-1))

        def mid(self):
            self.mid_up()
            self.mid_down()

        def end(self):
            self.up2.wait_recv()
            self.down2.wait_recv()

    def place(make, half, xx, first, second):
        return make(xx, y + first, z + second) if half == 0 else make(xx, y + second, z + first)

    def ring_first(half, xx):
        return (
            lambda o: place(spot, half, xx, o, 0),
            lambda o: place(idx, half, xh, o, 0),
        )

    def ring_second(half, xx, e):
        return (
            lambda o: place(spot, half, xx, e, o),
            lambda o: place(idx, half, xh, 0, o),
        )

    def line(half, xx, e):
        _, yy, zz = place(spot, half, xx, e, 0)
        return (xx, yy, slice(None)) if half == 0 else (xx, slice(None), zz)

    OFFS = (0, -1, 1, 2)
    own, peer = xh, 1 - xh

    class GatherSet:
        def __init__(self, xx, n):
            lanes = QW if n == 0 else QW - LX
            self.one = [
                Gather(ring_first(h, xx), 2 * h, 40 * n + 20 * h, lanes) for h in (0, 1)
            ]
            self.two = [
                {
                    e: Gather(
                        ring_second(h, xx, e), 2 * h, 40 * n + 20 * h + 4 + 4 * i, lanes
                    )
                    for i, e in enumerate(OFFS)
                }
                for h in (0, 1)
            ]

        def s1(self):
            for h in (0, 1):
                self.one[h].start()
            for h in (0, 1):
                self.two[h][0].start()

        def s2(self):
            for h in (0, 1):
                self.one[h].mid_up()
                self.two[h][-1].start()
                self.one[h].mid_down()
                self.two[h][1].start()

        def mid(self, e):
            for h in (0, 1):
                self.two[h][e].mid()

        def s4(self):
            for h in (0, 1):
                self.one[h].end()
                self.two[h][2].start()

        def end(self, e):
            for h in (0, 1):
                self.two[h][e].end()

    far = idx(peer, y, z)
    row16 = lax.broadcasted_iota(jnp.int32, (256, 1), 0) & 3

    def project(xx):
        def lhs(q, a=0, b=QW):
            return xg[q, xx, :, :, :, a:b].reshape(256, b - a)

        def dot(l, a, b):
            return lax.dot_general(
                l, wq[:, a:b], (((1,), (1,)), ((), ())), preferred_element_type=F32
            )

        m = MAIN
        main = dot(lhs(0), 0, QW)
        for q in (1, 2, 3):
            main = main + dot(lhs(q), q * QW, (q + 1) * QW)
        tails = (
            dot(lhs(0), m, m + 1536) + dot(lhs(1, 0, 512), m + 1536, m + 2048),
            dot(lhs(1, 512, 1536), m, m + 1024) + dot(lhs(2, 0, 1024), m + 1024, m + 2048),
            dot(lhs(2, 1024, 1536), m, m + 512) + dot(lhs(3), m + 512, m + 2048),
        )
        add = jnp.zeros_like(main)
        for s in range(3):
            qacc[:, 0:320] = tails[s]
            add = jnp.where(row16 == s, pltpu.roll(qacc[...], 256 - (3 - s), 0)[:, 0:320], add)
        qacc[:, 0:320] = main + add
        qacc[:, 320:384] = jnp.zeros((256, 64), F32)
        flat = qacc[...]
        odd = lax.rem(t, 2) == 1
        full = jnp.where(odd, pltpu.roll(flat, 320, 1)[:, 0:256], flat[:, 0:256])
        part = jnp.where(odd, flat[:, 0:128], flat[:, 256:384])
        lane = lax.broadcasted_iota(jnp.int32, (256, 128), 1)
        left = jnp.where(
            lane < 64, pltpu.roll(part, 3, 0), pltpu.roll(pltpu.roll(part, 2, 0), 64, 1)
        )
        right = pltpu.roll(part, 1, 0)
        both = jnp.where(row16 == 3, jnp.concatenate([left, right], axis=1), full)
        qout[pl.ds(xx * 16, 16)] = both.reshape(16, 16, 256).astype(BF16)

    def a2a(src, dst, base, to):
        return pltpu.make_async_remote_copy(
            src_ref=src, dst_ref=dst.at[t],
            send_sem=as_sem.at[base + to], recv_sem=ar_sem.at[base + t],
            device_id=(g, to), device_id_type=MESH,
        )

    def a2a_wait(src, dst, base):
        def one(i, c):
            fr = lax.rem(t + i, N_T)
            d = pltpu.make_async_remote_copy(
                src_ref=src.at[fr], dst_ref=dst.at[fr],
                send_sem=as_sem.at[base + fr], recv_sem=ar_sem.at[base + fr],
                device_id=(g, fr), device_id_type=MESH,
            )
            d.wait_recv()
            d.wait_send()
            return c

        lax.fori_loop(1, N_T, one, 0)

    near_set, far_set = GatherSet(own, 0), GatherSet(peer, 1)

    def across(e):
        got = []
        for h in (0, 1):
            near_set.two[h][e].end()
            ref = xg.at[(pl.ds(2 * h, 2), *line(h, own, e), slice(None), pl.ds(QW - LX, LX))]
            got.append(send(ref, ref, 242 + 2 * OFFS.index(e) + h, far))
        return got

    near_set.s1()
    mine = xg.at[:, xh, y, z, :, 0 : QW - LX]
    over = [send(mine, mine, 160, far)]
    near_set.s2()
    near_set.mid(0)
    near_set.s4()
    over[0].wait_recv()
    far_set.s1()
    near_set.mid(-1)
    near_set.mid(1)
    over += across(0)
    far_set.s2()
    near_set.mid(2)
    for e in (-1, 1, 2):
        over += across(e)
    far_set.mid(0)
    far_set.s4()
    far_set.mid(-1)
    far_set.mid(1)
    loads[0].wait()
    project(own)

    def send_near(i, c):
        to = own * 16 + lax.rem(t + i, 16)
        a2a(qout.at[to], qin, 0, to).start()
        return c

    lax.fori_loop(1, 16, send_near, 0)
    qin[t] = qout[t]
    far_set.mid(2)
    for e in OFFS:
        far_set.end(e)
    for c in over[1:]:
        c.wait_recv()
    project(peer)

    def send_far(i, c):
        to = peer * 16 + lax.rem(t + i, 16)
        a2a(qout.at[to], qin, 0, to).start()
        return c

    lax.fori_loop(0, 16, send_far, 0)

    used = [(lens[0, j] + 127) // 128 for j in range(4)]
    first = [0, used[0], used[0] + used[1], used[0] + used[1] + used[2]]

    def of_group(values, gg):
        total = jnp.int32(0)
        for j in range(4):
            total = total + jnp.where(mig[0, j] == gg, values[j], 0)
        return total

    row_len = [of_group([lens[0, j] for j in range(4)], gg) for gg in range(N_G)]
    pages = [
        [order[0, jnp.clip(of_group(first, gg) + b, 0, 11)] for b in range(4)]
        for gg in range(N_G)
    ]

    def by_row(rows, values):
        kind = (rows & 15) >> 2
        got = jnp.where(kind == 0, values[0], values[1])
        got = jnp.where(kind == 2, values[2], got)
        return jnp.where(kind == 3, values[3], got)

    r16 = lax.broadcasted_iota(jnp.int32, (16, 128), 0)
    angle = (by_row(r16, row_len) + (r16 & 3)).astype(F32) * inv[...]
    lane16 = lax.broadcasted_iota(jnp.int32, (16, 128), 1)
    cosine = jnp.cos(angle)
    sine = jnp.where(lane16 < 64, -jnp.sin(angle), jnp.sin(angle))

    a2a_wait(qout, qin, 0)

    def unpack(block):
        one, two = block[:, 0:128], block[:, 128:256]
        step = r16 & 3
        half = jnp.where(
            step == 0, pltpu.roll(one, 13, 0), pltpu.roll(pltpu.roll(one, 14, 0), 64, 1)
        )
        return one, two, jnp.where(step == 2, pltpu.roll(two, 15, 0), half)

    def pair(p, c):
        e0, e1, low = unpack(qin[2 * p].astype(F32))
        o0, o1, high = unpack(qin[2 * p + 1].astype(F32))
        five = (e0, e1, jnp.where(lane16 < 64, low, pltpu.roll(high, 64, 1)), o0, o1)
        for i, h in enumerate(five):
            turned = h * cosine + pltpu.roll(h, 64, 1) * sine
            heads[5 * p + i] = jnp.where(5 * p + i < 72, turned, h).astype(BF16)
        return c

    lax.fori_loop(0, 16, pair, 0)

    loads[1].wait()
    r128 = lax.broadcasted_iota(jnp.int32, (128, 128), 0)
    c128 = lax.broadcasted_iota(jnp.int32, (128, 128), 1)
    r512 = lax.broadcasted_iota(jnp.int32, (128, 512), 0)
    c512 = lax.broadcasted_iota(jnp.int32, (128, 512), 1)
    lim = by_row(lax.broadcasted_iota(jnp.int32, (128, 1), 0), row_len)
    fresh = (
        (c128 < 16) & ((c128 >> 2) == ((r128 & 15) >> 2)) & ((c128 & 3) <= (r128 & 3))
    )
    pad = jnp.zeros((112, 128), BF16)

    def attend(k, c):
        queries = heads[pl.ds(8 * k, 8)].reshape(128, 128)

        def scores(keys):
            return lax.dot_general(
                queries, keys, (((1,), (1,)), ((), ())), preferred_element_type=F32
            )

        def page(gg, b, what):
            return kv[pages[gg][b], what, k]

        cached = [
            scores(jnp.concatenate([page(gg, b, 0) for b in range(4)], axis=0))
            for gg in range(N_G)
        ]
        cached = by_row(r512, cached) * SCALE
        live = c512 < lim
        cached = jnp.where(live, cached, NEG_FILL)
        newest = scores(jnp.concatenate([heads[64 + k], pad], axis=0)) * SCALE
        newest = jnp.where(fresh, newest, NEG_FILL)
        top = jnp.maximum(
            jnp.max(cached, axis=-1, keepdims=True), jnp.max(newest, axis=-1, keepdims=True)
        )
        weights = jnp.where(live, jnp.exp(cached - top), 0.0).astype(BF16)
        extra = jnp.where(fresh, jnp.exp(newest - top), 0.0).astype(BF16)
        total = jnp.sum(weights.astype(F32), axis=-1, keepdims=True) + jnp.sum(
            extra.astype(F32), axis=-1, keepdims=True
        )
        acc = []
        for pair_of in ((0, 1), (2, 3)):
            values = jnp.concatenate(
                [
                    jnp.concatenate([page(gg, b, 1) for b in range(4)], axis=0)
                    for gg in pair_of
                ],
                axis=1,
            )
            two = jnp.dot(weights, values, preferred_element_type=F32)
            acc += [two[:, 0:128], two[:, 128:256]]
        acc = by_row(r128, acc) + jnp.dot(
            extra,
            jnp.concatenate([heads[72 + k], pad], axis=0),
            preferred_element_type=F32,
        )
        att[pl.ds(4 * k, 4)] = (acc / total).reshape(4, 2, 16, 128).astype(BF16)

        def give(i, c):
            to = 4 * k + i

            @pl.when(to != t)
            def _():
                a2a(att.at[to], ain, N_T, to).start()

            return c

        lax.fori_loop(0, 4, give, 0)
        return c

    lax.fori_loop(0, 8, attend, 0, unroll=2)
    ain[t] = att[t]
    loads[2].wait()
    a2a_wait(att, ain, N_T)

    def lhs_of(xx):
        left = jnp.concatenate(
            [ain[pl.ds(xx * 16, 16), i].reshape(256, 128) for i in (0, 1)], axis=1
        )
        wide = left.astype(F32)
        return left, [pltpu.roll(wide, 3 - s, 0).astype(BF16) for s in range(3)]

    def expand(sides, xx, half):
        left, turned = sides
        for c in range(6 * half, 6 * half + 6):
            at = MAIN + (c % 4) * CHUNK
            main = jnp.dot(
                left, wo[:, c * CHUNK : (c + 1) * CHUNK], preferred_element_type=F32
            )
            tail = jnp.dot(turned[c // 4], wo[:, at : at + CHUNK], preferred_element_type=F32)
            lane = (c % 3) * CHUNK
            terms[c // 3, xx, :, :, :, lane : lane + CHUNK] = (
                jnp.where(row16 == 3, tail, main).reshape(4, 4, 16, CHUNK).astype(BF16)
            )

    class Reduce:
        def __init__(self, at, q, k, n, lanes):
            self.at, self.to = at
            self.q, self.k, self.n = q, k, n
            self.lanes = slice(0, lanes)

        def part(self, o, i):
            return (self.q + i, *self.at(o), slice(None), self.lanes)

        def both(self, o):
            return (pl.ds(self.q, 2), *self.at(o), slice(None), self.lanes)

        def s1(self):
            k, n, w = self.k, self.n, self.lanes
            self.up = send(terms.at[self.part(2, 0)], rq.at[n, 0, :, w], k, self.to(1))
            self.down = send(terms.at[self.part(-2, 1)], rq.at[n, 1, :, w], k + 1, self.to(-1))

        def s2(self):
            k, n, w = self.k, self.n, self.lanes
            for i, d, came in ((0, 1, self.up), (1, -1, self.down)):
                came.wait_recv()
                p = self.part(d, i)
                terms[p] = (terms[p].astype(F32) + rq[n, i, :, w].astype(F32)).astype(BF16)
                on = send(
                    terms.at[self.both(d)], rf.at[n, i, :, :, w], k + 2 + i, self.to(d)
                )
                if i == 0:
                    self.up2 = on
                else:
                    self.down2 = on

        def s3(self):
            n, w = self.n, self.lanes
            self.up2.wait_recv()
            self.down2.wait_recv()
            for i in (0, 1):
                p = self.part(0, i)
                terms[p] = (
                    terms[p].astype(F32)
                    + rf[n, 0, i, :, w].astype(F32)
                    + rf[n, 1, i, :, w].astype(F32)
                ).astype(BF16)

    class ReduceSet:
        def __init__(self, xx, n):
            k, m = 161 + 40 * n, 10 * n
            lanes = QW - LX if n == 0 else QW
            self.big = [
                {
                    e: Reduce(
                        ring_second(h, xx, e), 2 * h, k + 20 * h + 4 * i, m + 5 * h + i, lanes
                    )
                    for i, e in enumerate(OFFS)
                }
                for h in (0, 1)
            ]
            self.last = [
                Reduce(ring_first(h, xx), 2 * h, k + 20 * h + 16, m + 5 * h + 4, lanes)
                for h in (0, 1)
            ]

        def s1(self, h, *es):
            for e in es:
                self.big[h][e].s1()

        def s2(self, *es):
            for e in es:
                for h in (0, 1):
                    self.big[h][e].s2()

        def s3(self, *es):
            for e in es:
                for h in (0, 1):
                    self.big[h][e].s3()

        def l1(self):
            for h in (0, 1):
                self.last[h].s1()

        def l2(self):
            for h in (0, 1):
                self.last[h].s2()

        def l3(self):
            for h in (0, 1):
                self.last[h].s3()

    far_sum, near_sum = ReduceSet(peer, 0), ReduceSet(own, 1)
    BACK = (2, -1, 1, 0)
    cross = {}

    def hand(h):
        for i, e in enumerate(BACK):
            lanes = pl.ds(QW - LX, LX)
            _, yy, zz = line(h, peer, e)
            cross[h, e] = send(
                terms.at[pl.ds(2 * h, 2), peer, yy, zz, :, lanes],
                rc.at[pl.ds(2 * h, 2), yy, zz],
                250 + 4 * h + i,
                far,
            )

    def take(h, e):
        cross[h, e].wait_recv()
        for q in (2 * h, 2 * h + 1):
            for o in range(4):
                _, yy, zz = place(spot, h, own, e, o)
                old = terms[q, own, yy, zz, :, QW - LX : QW].astype(F32)
                terms[q, own, yy, zz, :, QW - LX : QW] = (
                    old + rc[q, yy, zz].astype(F32)
                ).astype(BF16)
        near_sum.s1(h, e)

    sides = lhs_of(peer)
    expand(sides, peer, 0)
    far_sum.s1(0, *BACK)
    hand(0)
    expand(sides, peer, 1)
    far_sum.s1(1, *BACK)
    hand(1)
    far_sum.s2(*BACK)
    sides = lhs_of(own)
    expand(sides, own, 0)
    expand(sides, own, 1)
    take(0, 2)
    take(1, 2)
    far_sum.s3(2)
    far_sum.l1()
    take(0, -1)
    take(1, -1)
    near_sum.s2(2)
    far_sum.s3(-1, 1)
    far_sum.l2()
    take(0, 1)
    take(1, 1)
    near_sum.s2(-1)
    far_sum.s3(0)
    far_sum.l3()
    over = send(terms.at[:, peer, y, z, :, 0 : QW - LX], rx, 241, far)
    take(0, 0)
    take(1, 0)
    near_sum.s2(1)
    near_sum.s3(2)
    near_sum.l1()
    near_sum.s2(0)
    near_sum.s3(-1, 1)
    near_sum.l2()
    near_sum.s3(0)
    near_sum.l3()
    over.wait_recv()
    for q in range(4):
        x32[q, :, 0 : QW - LX] = terms[q, xh, y, z, :, 0 : QW - LX].astype(F32) + rx[q].astype(F32)
        x32[q, :, QW - LX : QW] = terms[q, xh, y, z, :, QW - LX : QW].astype(F32)
    for gg in range(N_G):
        for q in range(4):
            stage[gg, 4 * q : 4 * q + 4, :] = x32[q, 4 * gg : 4 * gg + 4, :]
    for gg in range(N_G):
        fsend[gg] = stage[gg].astype(BF16)
    sent.extend(group_exchange(fsend, frecv, N_G))
    for s in range(N_G):
        stage[s] = frecv[s].astype(F32)
        for j in range(3):
            for q in range(4):
                o32[j, s : s + 1, q * QW : (q + 1) * QW] = stage[
                    s, 4 * q + j : 4 * q + j + 1, :
                ]
            for c in range(4 * j, 4 * j + 4):
                at = MAIN + (c % 4) * CHUNK
                lane = (c % 3) * CHUNK
                row = 4 * (c // 3) + 3
                o32[j, s : s + 1, at : at + CHUNK] = stage[
                    s, row : row + 1, lane : lane + CHUNK
                ]
    for j in range(3):
        out[j] = o32[j].astype(BF16)
    for c in sent:
        c.wait_send()


def per_device(tokens, norm_gain, w_qkv, w_out, lengths, migrate, page_order, kv_pool):
    inverse = np.float32(ROPE_BASE) ** (-(np.arange(64, dtype=np.float32) * np.float32(2.0) / 128))
    inverse = jnp.asarray(np.concatenate([inverse, inverse]).reshape(1, 128), F32)
    vmem = pl.BlockSpec(memory_space=pltpu.VMEM)
    smem = pl.BlockSpec(memory_space=pltpu.SMEM)
    hbm = pl.BlockSpec(memory_space=pl.ANY)
    dma = pltpu.SemaphoreType.DMA
    done = pl.pallas_call(
        body,
        out_shape=jax.ShapeDtypeStruct((3, 4, D), BF16),
        in_specs=[vmem, vmem, smem, smem, smem, hbm, hbm, hbm, hbm],
        out_specs=vmem,
        scratch_shapes=[
            pltpu.VMEM((3, 4, D), BF16),
            pltpu.VMEM((4, 16, QW), F32),
            pltpu.VMEM((4, 16, QW), BF16),
            pltpu.VMEM((4, 16, QW), BF16),
            pltpu.VMEM((4, 16, QW), F32),
            pltpu.VMEM((4, 2, 4, 4, 16, QW), BF16),
            pltpu.VMEM((320, D), BF16),
            pltpu.VMEM((256, D), BF16),
            pltpu.VMEM((12, 2, 8, 128, 128), BF16),
            pltpu.VMEM((256, 384), F32),
            pltpu.VMEM((32, 16, 256), BF16),
            pltpu.VMEM((32, 16, 256), BF16),
            pltpu.VMEM((80, 16, 128), BF16),
            pltpu.VMEM((32, 2, 16, 128), BF16),
            pltpu.VMEM((32, 2, 16, 128), BF16),
            pltpu.VMEM((4, 2, 4, 4, 16, QW), BF16),
            pltpu.VMEM((20, 2, 16, QW), BF16),
            pltpu.VMEM((20, 2, 2, 16, QW), BF16),
            pltpu.VMEM((4, 16, QW - LX), BF16),
            pltpu.VMEM((4, 4, 4, 16, LX), BF16),
            pltpu.VMEM((4, 16, QW), BF16),
            pltpu.VMEM((4, 16, QW), BF16),
            pltpu.VMEM((3, 4, D), F32),
            dma((4,)),
            dma((2 * N_G,)),
            dma((2 * N_G,)),
            dma((258,)),
            dma((258,)),
            dma((2 * N_T,)),
            dma((2 * N_T,)),
        ],
        compiler_params=pltpu.CompilerParams(
            collective_id=0, has_side_effects=True, vmem_limit_bytes=60 * 2**20
        ),
        cost_estimate=pl.CostEstimate(
            flops=4 * 10**9, bytes_accessed=17 * 10**6, transcendentals=10**6
        ),
    )(
        norm_gain.reshape(1, D), inverse, lengths, migrate, page_order,
        tokens.transpose(1, 0, 2), w_qkv.T, w_out, kv_pool.reshape(12, 2, 8, 128, 128),
    )
    return (tokens.astype(F32) + done.transpose(1, 0, 2).astype(F32)).astype(BF16)


def solution(mesh):
    both = ("group", "tensor")
    return jax.shard_map(
        per_device,
        mesh=mesh,
        in_specs=(
            P(both, None, None),
            P(),
            P(None, "tensor"),
            P("tensor", None),
            P(both, None),
            P(both, None),
            P(both, None),
            P(both, None, None, None, None, None),
        ),
        out_specs=P(both, None, None),
        check_vma=False,
    )
```

```python
import jax
import jax.numpy as jnp
import numpy as np
from jax import lax
from jax.experimental import pallas as pl
from jax.experimental.pallas import tpu as pltpu
from jax.sharding import PartitionSpec as P

MESH = pl.DeviceIdType.MESH
F32 = jnp.float32
BF16 = jnp.bfloat16
EPS = 1e-05
ROPE_BASE = 500000.0
NEG_FILL = -1e30
SCALE = 128 ** (-0.5)
D = 8192
MAIN = 6144
QW = 1536
CHUNK = 512
LG = 256
LR = 256
N_T = 32
N_G = 4


def body(
    gain, inv, lens, mig, order, tok_hbm, wqkv_hbm, wout_hbm, kv_hbm, out,
    tok, stage, gsend, grecv, x32, xg, wq, wo, kv, qacc, qout, qin, heads, att, ain,
    terms, rq, rf, rx, rc, fsend, frecv, o32,
    load_sem, gs_sem, gr_sem, s_sem, r_sem, as_sem, ar_sem,
):
    g = lax.axis_index("group")
    t = lax.axis_index("tensor")
    xh, y, z = t // 16, (t // 4) % 4, t % 4

    def idx(xx, yy, zz):
        return xx * 16 + lax.rem(yy + 4, 4) * 4 + lax.rem(zz + 4, 4)

    def spot(xx, yy, zz):
        return xx, lax.rem(yy + 4, 4), lax.rem(zz + 4, 4)

    barrier = pltpu.get_barrier_semaphore()
    first_load = pltpu.make_async_copy(tok_hbm, tok, load_sem.at[3])
    first_load.start()

    near = [(g, idx(1 - xh, y, z))]
    near += [(g, idx(xh, y + d, z)) for d in (1, -1)]
    near += [(g, idx(xh, y, z + d)) for d in (1, -1)]
    near += [(lax.rem(g + i, N_G), t) for i in range(1, N_G)]
    for to in near:
        pl.semaphore_signal(barrier, inc=1, device_id=to, device_id_type=MESH)

    loads = [
        pltpu.make_async_copy(wqkv_hbm, wq, load_sem.at[0]),
        pltpu.make_async_copy(kv_hbm, kv, load_sem.at[1]),
        pltpu.make_async_copy(wout_hbm, wo, load_sem.at[2]),
    ]
    for c in loads:
        c.start()

    first_load.wait()
    for j in range(3):
        rows = tok[j].astype(F32)
        mean = jnp.mean(rows * rows, axis=-1, keepdims=True)
        normed = rows * lax.rsqrt(mean + EPS) * gain[...]
        for s in range(N_G):
            for q in range(4):
                stage[s, 4 * q + j : 4 * q + j + 1, :] = normed[
                    s : s + 1, q * QW : (q + 1) * QW
                ]
            for c in range(4 * j, 4 * j + 4):
                at = MAIN + (c % 4) * CHUNK
                lane = (c % 3) * CHUNK
                row = 4 * (c // 3) + 3
                stage[s, row : row + 1, lane : lane + CHUNK] = normed[
                    s : s + 1, at : at + CHUNK
                ]
    for s in range(N_G):
        gsend[s] = stage[s].astype(BF16)

    pl.semaphore_wait(barrier, len(near))

    def group_exchange(src, dst, base):
        copies = []
        for i in range(1, N_G):
            to = lax.rem(g + i, N_G)
            copies.append(
                pltpu.make_async_remote_copy(
                    src_ref=src.at[to], dst_ref=dst.at[g],
                    send_sem=gs_sem.at[base + i], recv_sem=gr_sem.at[base + i],
                    device_id=(to, t), device_id_type=MESH,
                )
            )
            copies[-1].start()
        dst[g] = src[g]
        for c in copies:
            c.wait_recv()
        return copies

    sent = group_exchange(gsend, grecv, 0)
    for gg in range(N_G):
        stage[gg] = grecv[gg].astype(F32)
    for gg in range(N_G):
        for q in range(4):
            x32[q, 4 * gg : 4 * gg + 4, :] = stage[gg, 4 * q : 4 * q + 4, :]
    for q in range(4):
        xg[q, xh, y, z] = x32[q].astype(BF16)

    def send(src, dst, k, to):
        c = pltpu.make_async_remote_copy(
            src_ref=src, dst_ref=dst, send_sem=s_sem.at[k], recv_sem=r_sem.at[k],
            device_id=(g, to), device_id_type=MESH,
        )
        c.start()
        sent.append(c)
        return c

    class Gather:
        def __init__(self, at, q, k, lanes):
            (self.at, self.to), self.q, self.k = at, q, k
            self.lanes = slice(0, lanes)

        def block(self, o, one=None):
            if one is None:
                return xg.at[(pl.ds(self.q, 2), *self.at(o), slice(None), self.lanes)]
            return xg.at[(self.q + one, *self.at(o), slice(None), self.lanes)]

        def start(self):
            ref = self.block(0)
            self.up = send(ref, ref, self.k, self.to(1))
            self.down = send(ref, ref, self.k + 1, self.to(-1))

        def mid_up(self):
            self.up.wait_recv()
            ref = self.block(-1, 0)
            self.up2 = send(ref, ref, self.k + 2, self.to(1))

        def mid_down(self):
            self.down.wait_recv()
            ref = self.block(1, 1)
            self.down2 = send(ref, ref, self.k + 3, self.to(-1))

        def mid(self):
            self.mid_up()
            self.mid_down()

        def end(self):
            self.up2.wait_recv()
            self.down2.wait_recv()

    def place(make, half, xx, first, second):
        return make(xx, y + first, z + second) if half == 0 else make(xx, y + second, z + first)

    def ring_first(half, xx):
        return (
            lambda o: place(spot, half, xx, o, 0),
            lambda o: place(idx, half, xh, o, 0),
        )

    def ring_second(half, xx, e):
        return (
            lambda o: place(spot, half, xx, e, o),
            lambda o: place(idx, half, xh, 0, o),
        )

    def line(half, xx, e):
        _, yy, zz = place(spot, half, xx, e, 0)
        return (xx, yy, slice(None)) if half == 0 else (xx, slice(None), zz)

    OFFS = (0, -1, 1, 2)
    own, peer = xh, 1 - xh

    class GatherSet:
        def __init__(self, xx, n):
            lanes = QW if n == 0 else QW - LG
            self.one = [
                Gather(ring_first(h, xx), 2 * h, 40 * n + 20 * h, lanes) for h in (0, 1)
            ]
            self.two = [
                {
                    e: Gather(
                        ring_second(h, xx, e), 2 * h, 40 * n + 20 * h + 4 + 4 * i, lanes
                    )
                    for i, e in enumerate(OFFS)
                }
                for h in (0, 1)
            ]

        def s1(self):
            for h in (0, 1):
                self.one[h].start()
            for h in (0, 1):
                self.two[h][0].start()

        def s2(self):
            for h in (0, 1):
                self.one[h].mid_up()
                self.two[h][-1].start()
                self.one[h].mid_down()
                self.two[h][1].start()

        def mid(self, e):
            for h in (0, 1):
                self.two[h][e].mid()

        def s4(self):
            for h in (0, 1):
                self.one[h].end()
                self.two[h][2].start()

        def end(self, e):
            for h in (0, 1):
                self.two[h][e].end()

    far = idx(peer, y, z)
    row16 = lax.broadcasted_iota(jnp.int32, (256, 1), 0) & 3

    def project(xx):
        def lhs(q, a=0, b=QW):
            return xg[q, xx, :, :, :, a:b].reshape(256, b - a)

        def dot(l, a, b):
            return lax.dot_general(
                l, wq[:, a:b], (((1,), (1,)), ((), ())), preferred_element_type=F32
            )

        m = MAIN
        main = dot(lhs(0), 0, QW)
        for q in (1, 2, 3):
            main = main + dot(lhs(q), q * QW, (q + 1) * QW)
        tails = (
            dot(lhs(0), m, m + 1536) + dot(lhs(1, 0, 512), m + 1536, m + 2048),
            dot(lhs(1, 512, 1536), m, m + 1024) + dot(lhs(2, 0, 1024), m + 1024, m + 2048),
            dot(lhs(2, 1024, 1536), m, m + 512) + dot(lhs(3), m + 512, m + 2048),
        )
        add = jnp.zeros_like(main)
        for s in range(3):
            qacc[:, 0:320] = tails[s]
            add = jnp.where(row16 == s, pltpu.roll(qacc[...], 256 - (3 - s), 0)[:, 0:320], add)
        qacc[:, 0:320] = main + add
        qacc[:, 320:384] = jnp.zeros((256, 64), F32)
        flat = qacc[...]
        odd = lax.rem(t, 2) == 1
        full = jnp.where(odd, pltpu.roll(flat, 320, 1)[:, 0:256], flat[:, 0:256])
        part = jnp.where(odd, flat[:, 0:128], flat[:, 256:384])
        lane = lax.broadcasted_iota(jnp.int32, (256, 128), 1)
        left = jnp.where(
            lane < 64, pltpu.roll(part, 3, 0), pltpu.roll(pltpu.roll(part, 2, 0), 64, 1)
        )
        right = pltpu.roll(part, 1, 0)
        both = jnp.where(row16 == 3, jnp.concatenate([left, right], axis=1), full)
        qout[pl.ds(xx * 16, 16)] = both.reshape(16, 16, 256).astype(BF16)

    def a2a(src, dst, which, to):
        return pltpu.make_async_remote_copy(
            src_ref=src, dst_ref=dst.at[t],
            send_sem=as_sem.at[which], recv_sem=ar_sem.at[which],
            device_id=(g, to), device_id_type=MESH,
        )

    def a2a_wait(src, dst, which):
        all_of = pltpu.make_async_remote_copy(
            src_ref=src.at[pl.ds(0, N_T - 1)], dst_ref=dst.at[pl.ds(0, N_T - 1)],
            send_sem=as_sem.at[which], recv_sem=ar_sem.at[which],
            device_id=(g, far), device_id_type=MESH,
        )
        all_of.wait_recv()
        sent.append(all_of)

    near_set, far_set = GatherSet(own, 0), GatherSet(peer, 1)

    def across(e):
        got = []
        for h in (0, 1):
            near_set.two[h][e].end()
            ref = xg.at[(pl.ds(2 * h, 2), *line(h, own, e), slice(None), pl.ds(QW - LG, LG))]
            got.append(send(ref, ref, 242 + 2 * OFFS.index(e) + h, far))
        return got

    near_set.s1()
    mine = xg.at[:, xh, y, z, :, 0 : QW - LG]
    over = [send(mine, mine, 160, far)]
    near_set.s2()
    near_set.mid(0)
    near_set.s4()
    over[0].wait_recv()
    far_set.s1()
    near_set.mid(-1)
    near_set.mid(1)
    over += across(0)
    far_set.s2()
    near_set.mid(2)
    for e in (-1, 1, 2):
        over += across(e)
    far_set.mid(0)
    far_set.s4()
    far_set.mid(-1)
    far_set.mid(1)
    loads[0].wait()
    project(own)

    def send_near(i, c):
        to = own * 16 + lax.rem(t + i, 16)
        a2a(qout.at[to], qin, 0, to).start()
        return c

    lax.fori_loop(1, 16, send_near, 0)
    qin[t] = qout[t]
    far_set.mid(2)
    for e in OFFS:
        far_set.end(e)
    for c in over[1:]:
        c.wait_recv()
    project(peer)

    def send_far(i, c):
        to = peer * 16 + lax.rem(t + i, 16)
        a2a(qout.at[to], qin, 0, to).start()
        return c

    lax.fori_loop(0, 16, send_far, 0)

    used = [(lens[0, j] + 127) // 128 for j in range(4)]
    first = [0, used[0], used[0] + used[1], used[0] + used[1] + used[2]]

    def of_group(values, gg):
        total = jnp.int32(0)
        for j in range(4):
            total = total + jnp.where(mig[0, j] == gg, values[j], 0)
        return total

    row_len = [of_group([lens[0, j] for j in range(4)], gg) for gg in range(N_G)]
    pages = [
        [order[0, jnp.clip(of_group(first, gg) + b, 0, 11)] for b in range(4)]
        for gg in range(N_G)
    ]

    def by_row(rows, values):
        kind = (rows & 15) >> 2
        got = jnp.where(kind == 0, values[0], values[1])
        got = jnp.where(kind == 2, values[2], got)
        return jnp.where(kind == 3, values[3], got)

    r16 = lax.broadcasted_iota(jnp.int32, (16, 128), 0)
    angle = (by_row(r16, row_len) + (r16 & 3)).astype(F32) * inv[...]
    lane16 = lax.broadcasted_iota(jnp.int32, (16, 128), 1)
    cosine = jnp.cos(angle)
    sine = jnp.where(lane16 < 64, -jnp.sin(angle), jnp.sin(angle))

    a2a_wait(qout, qin, 0)

    def unpack(block):
        one, two = block[:, 0:128], block[:, 128:256]
        step = r16 & 3
        half = jnp.where(
            step == 0, pltpu.roll(one, 13, 0), pltpu.roll(pltpu.roll(one, 14, 0), 64, 1)
        )
        return one, two, jnp.where(step == 2, pltpu.roll(two, 15, 0), half)

    def pair(p, c):
        e0, e1, low = unpack(qin[2 * p].astype(F32))
        o0, o1, high = unpack(qin[2 * p + 1].astype(F32))
        five = (e0, e1, jnp.where(lane16 < 64, low, pltpu.roll(high, 64, 1)), o0, o1)
        for i, h in enumerate(five):
            turned = h * cosine + pltpu.roll(h, 64, 1) * sine
            heads[5 * p + i] = jnp.where(5 * p + i < 72, turned, h).astype(BF16)
        return c

    lax.fori_loop(0, 16, pair, 0)

    loads[1].wait()
    r128 = lax.broadcasted_iota(jnp.int32, (128, 128), 0)
    c128 = lax.broadcasted_iota(jnp.int32, (128, 128), 1)
    r512 = lax.broadcasted_iota(jnp.int32, (128, 512), 0)
    c512 = lax.broadcasted_iota(jnp.int32, (128, 512), 1)
    lim = by_row(lax.broadcasted_iota(jnp.int32, (128, 1), 0), row_len)
    fresh = (
        (c128 < 16) & ((c128 >> 2) == ((r128 & 15) >> 2)) & ((c128 & 3) <= (r128 & 3))
    )
    pad = jnp.zeros((112, 128), BF16)

    def attend(i, c):
        k = lax.rem(i + 4 * peer, 8)
        queries = heads[pl.ds(8 * k, 8)].reshape(128, 128)

        def scores(keys):
            return lax.dot_general(
                queries, keys, (((1,), (1,)), ((), ())), preferred_element_type=F32
            )

        def page(gg, b, what):
            return kv[pages[gg][b], what, k]

        cached = [
            scores(jnp.concatenate([page(gg, b, 0) for b in range(4)], axis=0))
            for gg in range(N_G)
        ]
        cached = by_row(r512, cached) * SCALE
        live = c512 < lim
        cached = jnp.where(live, cached, NEG_FILL)
        newest = scores(jnp.concatenate([heads[64 + k], pad], axis=0)) * SCALE
        newest = jnp.where(fresh, newest, NEG_FILL)
        top = jnp.maximum(
            jnp.max(cached, axis=-1, keepdims=True), jnp.max(newest, axis=-1, keepdims=True)
        )
        weights = jnp.where(live, jnp.exp(cached - top), 0.0).astype(BF16)
        extra = jnp.where(fresh, jnp.exp(newest - top), 0.0).astype(BF16)
        total = jnp.sum(weights.astype(F32), axis=-1, keepdims=True) + jnp.sum(
            extra.astype(F32), axis=-1, keepdims=True
        )
        acc = []
        for pair_of in ((0, 1), (2, 3)):
            values = jnp.concatenate(
                [
                    jnp.concatenate([page(gg, b, 1) for b in range(4)], axis=0)
                    for gg in pair_of
                ],
                axis=1,
            )
            two = jnp.dot(weights, values, preferred_element_type=F32)
            acc += [two[:, 0:128], two[:, 128:256]]
        acc = by_row(r128, acc) + jnp.dot(
            extra,
            jnp.concatenate([heads[72 + k], pad], axis=0),
            preferred_element_type=F32,
        )
        att[pl.ds(4 * k, 4)] = (acc / total).reshape(4, 2, 16, 128).astype(BF16)

        def give(i, c):
            to = 4 * k + i

            @pl.when(to != t)
            def _():
                a2a(att.at[to], ain, 1, to).start()

            return c

        lax.fori_loop(0, 4, give, 0)
        return c

    lax.fori_loop(0, 8, attend, 0, unroll=2)
    ain[t] = att[t]
    loads[2].wait()
    a2a_wait(att, ain, 1)

    def lhs_of(xx):
        left = jnp.concatenate(
            [ain[pl.ds(xx * 16, 16), i].reshape(256, 128) for i in (0, 1)], axis=1
        )
        wide = left.astype(F32)
        return left, [pltpu.roll(wide, 3 - s, 0).astype(BF16) for s in range(3)]

    def expand(sides, xx, q):
        left, turned = sides
        for c in range(3 * q, 3 * q + 3):
            at = MAIN + (c % 4) * CHUNK
            main = jnp.dot(
                left, wo[:, c * CHUNK : (c + 1) * CHUNK], preferred_element_type=F32
            )
            tail = jnp.dot(turned[c // 4], wo[:, at : at + CHUNK], preferred_element_type=F32)
            lane = (c % 3) * CHUNK
            terms[c // 3, xx, :, :, :, lane : lane + CHUNK] = (
                jnp.where(row16 == 3, tail, main).reshape(4, 4, 16, CHUNK).astype(BF16)
            )

    class Reduce:
        def __init__(self, at, q, k, n, lanes):
            self.at, self.to = at
            self.q, self.k, self.n = q, k, n
            self.lanes = slice(0, lanes)

        def part(self, o, i):
            return (self.q + i, *self.at(o), slice(None), self.lanes)

        def both(self, o):
            return (pl.ds(self.q, 2), *self.at(o), slice(None), self.lanes)

        def s1(self, i):
            k, n, w = self.k, self.n, self.lanes
            if i == 0:
                self.up = send(terms.at[self.part(2, 0)], rq.at[n, 0, :, w], k, self.to(1))
            else:
                self.down = send(
                    terms.at[self.part(-2, 1)], rq.at[n, 1, :, w], k + 1, self.to(-1)
                )

        def s2(self):
            k, n, w = self.k, self.n, self.lanes
            for i, d, came in ((0, 1, self.up), (1, -1, self.down)):
                came.wait_recv()
                p = self.part(d, i)
                terms[p] = (terms[p].astype(F32) + rq[n, i, :, w].astype(F32)).astype(BF16)
                on = send(
                    terms.at[self.both(d)], rf.at[n, i, :, :, w], k + 2 + i, self.to(d)
                )
                if i == 0:
                    self.up2 = on
                else:
                    self.down2 = on

        def s3(self):
            n, w = self.n, self.lanes
            self.up2.wait_recv()
            self.down2.wait_recv()
            for i in (0, 1):
                p = self.part(0, i)
                terms[p] = (
                    terms[p].astype(F32)
                    + rf[n, 0, i, :, w].astype(F32)
                    + rf[n, 1, i, :, w].astype(F32)
                ).astype(BF16)

    class ReduceSet:
        def __init__(self, xx, n):
            k, m = 161 + 40 * n, 10 * n
            lanes = QW - LR if n == 0 else QW
            self.big = [
                {
                    e: Reduce(
                        ring_second(h, xx, e), 2 * h, k + 20 * h + 4 * i, m + 5 * h + i, lanes
                    )
                    for i, e in enumerate(OFFS)
                }
                for h in (0, 1)
            ]
            self.last = [
                Reduce(ring_first(h, xx), 2 * h, k + 20 * h + 16, m + 5 * h + 4, lanes)
                for h in (0, 1)
            ]

        def s1(self, h, i, *es):
            for e in es:
                self.big[h][e].s1(i)

        def s2(self, *es):
            for e in es:
                for h in (0, 1):
                    self.big[h][e].s2()

        def s3(self, *es):
            for e in es:
                for h in (0, 1):
                    self.big[h][e].s3()

        def l1(self):
            for h in (0, 1):
                self.last[h].s1(0)
                self.last[h].s1(1)

        def l2(self):
            for h in (0, 1):
                self.last[h].s2()

        def l3(self):
            for h in (0, 1):
                self.last[h].s3()

    far_sum, near_sum = ReduceSet(peer, 0), ReduceSet(own, 1)
    BACK = (2, -1, 1, 0)
    cross = {}

    def hand(h):
        for i, e in enumerate(BACK):
            lanes = pl.ds(QW - LR, LR)
            _, yy, zz = line(h, peer, e)
            cross[h, e] = send(
                terms.at[pl.ds(2 * h, 2), peer, yy, zz, :, lanes],
                rc.at[pl.ds(2 * h, 2), yy, zz],
                250 + 4 * h + i,
                far,
            )

    def take(h, e):
        cross[h, e].wait_recv()
        for q in (2 * h, 2 * h + 1):
            for o in range(4):
                _, yy, zz = place(spot, h, own, e, o)
                old = terms[q, own, yy, zz, :, QW - LR : QW].astype(F32)
                terms[q, own, yy, zz, :, QW - LR : QW] = (
                    old + rc[q, yy, zz].astype(F32)
                ).astype(BF16)
        near_sum.s1(h, 0, e)
        near_sum.s1(h, 1, e)

    sides = lhs_of(peer)
    for q in (0, 2, 1, 3):
        expand(sides, peer, q)
        far_sum.s1(q // 2, q % 2, *BACK)
    hand(0)
    hand(1)
    far_sum.s2(*BACK)
    sides = lhs_of(own)
    for q in range(4):
        expand(sides, own, q)
    take(0, 2)
    take(1, 2)
    far_sum.s3(2)
    far_sum.l1()
    take(0, -1)
    take(1, -1)
    near_sum.s2(2)
    far_sum.s3(-1, 1)
    far_sum.l2()
    take(0, 1)
    take(1, 1)
    near_sum.s2(-1)
    far_sum.s3(0)
    far_sum.l3()
    over = send(terms.at[:, peer, y, z, :, 0 : QW - LR], rx, 241, far)
    take(0, 0)
    take(1, 0)
    near_sum.s2(1)
    near_sum.s3(2)
    near_sum.l1()
    near_sum.s2(0)
    near_sum.s3(-1, 1)
    near_sum.l2()
    near_sum.s3(0)
    near_sum.l3()
    over.wait_recv()
    for q in range(4):
        x32[q, :, 0 : QW - LR] = terms[q, xh, y, z, :, 0 : QW - LR].astype(F32) + rx[q].astype(F32)
        x32[q, :, QW - LR : QW] = terms[q, xh, y, z, :, QW - LR : QW].astype(F32)
    for gg in range(N_G):
        for q in range(4):
            stage[gg, 4 * q : 4 * q + 4, :] = x32[q, 4 * gg : 4 * gg + 4, :]
    for gg in range(N_G):
        fsend[gg] = stage[gg].astype(BF16)
    sent.extend(group_exchange(fsend, frecv, N_G))
    for s in range(N_G):
        stage[s] = frecv[s].astype(F32)
        for j in range(3):
            for q in range(4):
                o32[j, s : s + 1, q * QW : (q + 1) * QW] = stage[
                    s, 4 * q + j : 4 * q + j + 1, :
                ]
            for c in range(4 * j, 4 * j + 4):
                at = MAIN + (c % 4) * CHUNK
                lane = (c % 3) * CHUNK
                row = 4 * (c // 3) + 3
                o32[j, s : s + 1, at : at + CHUNK] = stage[
                    s, row : row + 1, lane : lane + CHUNK
                ]
    for j in range(3):
        out[j] = o32[j].astype(BF16)
    for c in sent:
        c.wait_send()


def per_device(tokens, norm_gain, w_qkv, w_out, lengths, migrate, page_order, kv_pool):
    inverse = np.float32(ROPE_BASE) ** (-(np.arange(64, dtype=np.float32) * np.float32(2.0) / 128))
    inverse = jnp.asarray(np.concatenate([inverse, inverse]).reshape(1, 128), F32)
    vmem = pl.BlockSpec(memory_space=pltpu.VMEM)
    smem = pl.BlockSpec(memory_space=pltpu.SMEM)
    hbm = pl.BlockSpec(memory_space=pl.ANY)
    dma = pltpu.SemaphoreType.DMA
    done = pl.pallas_call(
        body,
        out_shape=jax.ShapeDtypeStruct((3, 4, D), BF16),
        in_specs=[vmem, vmem, smem, smem, smem, hbm, hbm, hbm, hbm],
        out_specs=vmem,
        scratch_shapes=[
            pltpu.VMEM((3, 4, D), BF16),
            pltpu.VMEM((4, 16, QW), F32),
            pltpu.VMEM((4, 16, QW), BF16),
            pltpu.VMEM((4, 16, QW), BF16),
            pltpu.VMEM((4, 16, QW), F32),
            pltpu.VMEM((4, 2, 4, 4, 16, QW), BF16),
            pltpu.VMEM((320, D), BF16),
            pltpu.VMEM((256, D), BF16),
            pltpu.VMEM((12, 2, 8, 128, 128), BF16),
            pltpu.VMEM((256, 384), F32),
            pltpu.VMEM((32, 16, 256), BF16),
            pltpu.VMEM((32, 16, 256), BF16),
            pltpu.VMEM((80, 16, 128), BF16),
            pltpu.VMEM((32, 2, 16, 128), BF16),
            pltpu.VMEM((32, 2, 16, 128), BF16),
            pltpu.VMEM((4, 2, 4, 4, 16, QW), BF16),
            pltpu.VMEM((20, 2, 16, QW), BF16),
            pltpu.VMEM((20, 2, 2, 16, QW), BF16),
            pltpu.VMEM((4, 16, QW - LR), BF16),
            pltpu.VMEM((4, 4, 4, 16, LR), BF16),
            pltpu.VMEM((4, 16, QW), BF16),
            pltpu.VMEM((4, 16, QW), BF16),
            pltpu.VMEM((3, 4, D), F32),
            dma((4,)),
            dma((2 * N_G,)),
            dma((2 * N_G,)),
            dma((258,)),
            dma((258,)),
            dma((2,)),
            dma((2,)),
        ],
        compiler_params=pltpu.CompilerParams(
            collective_id=0, has_side_effects=True, vmem_limit_bytes=60 * 2**20
        ),
        cost_estimate=pl.CostEstimate(
            flops=4 * 10**9, bytes_accessed=17 * 10**6, transcendentals=10**6
        ),
    )(
        norm_gain.reshape(1, D), inverse, lengths, migrate, page_order,
        tokens.transpose(1, 0, 2), w_qkv.T, w_out, kv_pool.reshape(12, 2, 8, 128, 128),
    )
    return (tokens.astype(F32) + done.transpose(1, 0, 2).astype(F32)).astype(BF16)


def solution(mesh):
    both = ("group", "tensor")
    return jax.shard_map(
        per_device,
        mesh=mesh,
        in_specs=(
            P(both, None, None),
            P(),
            P(None, "tensor"),
            P("tensor", None),
            P(both, None),
            P(both, None),
            P(both, None),
            P(both, None, None, None, None, None),
        ),
        out_specs=P(both, None, None),
        check_vma=False,
    )
```

```python
import jax
import jax.numpy as jnp
import numpy as np
from jax import lax
from jax.experimental import pallas as pl
from jax.experimental.pallas import tpu as pltpu
from jax.sharding import PartitionSpec as P

MESH = pl.DeviceIdType.MESH
F32 = jnp.float32
BF16 = jnp.bfloat16
EPS = 1e-05
ROPE_BASE = 500000.0
NEG_FILL = -1e30
SCALE = 128 ** (-0.5)
D = 8192
MAIN = 6144
QW = 1536
CHUNK = 512
LG = 256
LR = 256
N_T = 32
N_G = 4


def body(
    gain_hbm, inv_hbm, lens_hbm, mig_hbm, order_hbm, tok_hbm, wqkv_hbm, wout_hbm, kv_hbm, out,
    gain, inv, lens, mig, order, tok, stage, gsend, grecv, x32, xg, wq, wo, kv, qacc, qout, qin, heads, att, ain,
    terms, rq, rf, rx, rc, fsend, frecv, o32,
    load_sem, gs_sem, gr_sem, s_sem, r_sem, as_sem, ar_sem,
):
    g = lax.axis_index("group")
    t = lax.axis_index("tensor")
    xh, y, z = t // 16, (t // 4) % 4, t % 4

    def idx(xx, yy, zz):
        return xx * 16 + lax.rem(yy + 4, 4) * 4 + lax.rem(zz + 4, 4)

    def spot(xx, yy, zz):
        return xx, lax.rem(yy + 4, 4), lax.rem(zz + 4, 4)

    barrier = pltpu.get_barrier_semaphore()
    near = [(g, idx(1 - xh, y, z))]
    near += [(g, idx(xh, y + d, z)) for d in (1, -1)]
    near += [(g, idx(xh, y, z + d)) for d in (1, -1)]
    near += [(lax.rem(g + i, N_G), t) for i in range(1, N_G)]
    for to in near:
        pl.semaphore_signal(barrier, inc=1, device_id=to, device_id_type=MESH)

    first_loads = [
        pltpu.make_async_copy(a, b, load_sem.at[3 + i])
        for i, (a, b) in enumerate(
            (
                (tok_hbm, tok), (gain_hbm, gain), (inv_hbm, inv),
                (lens_hbm, lens), (mig_hbm, mig), (order_hbm, order),
            )
        )
    ]
    for c in first_loads:
        c.start()

    loads = [
        pltpu.make_async_copy(wqkv_hbm, wq, load_sem.at[0]),
        pltpu.make_async_copy(kv_hbm, kv, load_sem.at[1]),
        pltpu.make_async_copy(wout_hbm, wo, load_sem.at[2]),
    ]
    for c in loads:
        c.start()

    for c in first_loads:
        c.wait()
    for j in range(3):
        rows = tok[j].astype(F32)
        mean = jnp.mean(rows * rows, axis=-1, keepdims=True)
        normed = rows * lax.rsqrt(mean + EPS) * gain[...]
        for s in range(N_G):
            for q in range(4):
                stage[s, 4 * q + j : 4 * q + j + 1, :] = normed[
                    s : s + 1, q * QW : (q + 1) * QW
                ]
            for c in range(4 * j, 4 * j + 4):
                at = MAIN + (c % 4) * CHUNK
                lane = (c % 3) * CHUNK
                row = 4 * (c // 3) + 3
                stage[s, row : row + 1, lane : lane + CHUNK] = normed[
                    s : s + 1, at : at + CHUNK
                ]
    for s in range(N_G):
        gsend[s] = stage[s].astype(BF16)

    pl.semaphore_wait(barrier, len(near))

    def group_exchange(src, dst, base):
        copies = []
        for i in range(1, N_G):
            to = lax.rem(g + i, N_G)
            copies.append(
                pltpu.make_async_remote_copy(
                    src_ref=src.at[to], dst_ref=dst.at[g],
                    send_sem=gs_sem.at[base + i], recv_sem=gr_sem.at[base + i],
                    device_id=(to, t), device_id_type=MESH,
                )
            )
            copies[-1].start()
        dst[g] = src[g]
        for c in copies:
            c.wait_recv()
        return copies

    sent = group_exchange(gsend, grecv, 0)
    for gg in range(N_G):
        stage[gg] = grecv[gg].astype(F32)
    for gg in range(N_G):
        for q in range(4):
            x32[q, 4 * gg : 4 * gg + 4, :] = stage[gg, 4 * q : 4 * q + 4, :]
    for q in range(4):
        xg[q, xh, y, z] = x32[q].astype(BF16)

    def send(src, dst, k, to):
        c = pltpu.make_async_remote_copy(
            src_ref=src, dst_ref=dst, send_sem=s_sem.at[k], recv_sem=r_sem.at[k],
            device_id=(g, to), device_id_type=MESH,
        )
        c.start()
        sent.append(c)
        return c

    class Gather:
        def __init__(self, at, q, k, lanes):
            (self.at, self.to), self.q, self.k = at, q, k
            self.lanes = slice(0, lanes)

        def block(self, o, one=None):
            if one is None:
                return xg.at[(pl.ds(self.q, 2), *self.at(o), slice(None), self.lanes)]
            return xg.at[(self.q + one, *self.at(o), slice(None), self.lanes)]

        def start(self):
            ref = self.block(0)
            self.up = send(ref, ref, self.k, self.to(1))
            self.down = send(ref, ref, self.k + 1, self.to(-1))

        def mid_up(self):
            self.up.wait_recv()
            ref = self.block(-1, 0)
            self.up2 = send(ref, ref, self.k + 2, self.to(1))

        def mid_down(self):
            self.down.wait_recv()
            ref = self.block(1, 1)
            self.down2 = send(ref, ref, self.k + 3, self.to(-1))

        def mid(self):
            self.mid_up()
            self.mid_down()

        def end(self):
            self.up2.wait_recv()
            self.down2.wait_recv()

    def place(make, half, xx, first, second):
        return make(xx, y + first, z + second) if half == 0 else make(xx, y + second, z + first)

    def ring_first(half, xx):
        return (
            lambda o: place(spot, half, xx, o, 0),
            lambda o: place(idx, half, xh, o, 0),
        )

    def ring_second(half, xx, e):
        return (
            lambda o: place(spot, half, xx, e, o),
            lambda o: place(idx, half, xh, 0, o),
        )

    def line(half, xx, e):
        _, yy, zz = place(spot, half, xx, e, 0)
        return (xx, yy, slice(None)) if half == 0 else (xx, slice(None), zz)

    OFFS = (0, -1, 1, 2)
    own, peer = xh, 1 - xh

    class GatherSet:
        def __init__(self, xx, n):
            lanes = QW if n == 0 else QW - LG
            self.one = [
                Gather(ring_first(h, xx), 2 * h, 40 * n + 20 * h, lanes) for h in (0, 1)
            ]
            self.two = [
                {
                    e: Gather(
                        ring_second(h, xx, e), 2 * h, 40 * n + 20 * h + 4 + 4 * i, lanes
                    )
                    for i, e in enumerate(OFFS)
                }
                for h in (0, 1)
            ]

        def s1(self):
            for h in (0, 1):
                self.one[h].start()
            for h in (0, 1):
                self.two[h][0].start()

        def s2(self):
            for h in (0, 1):
                self.one[h].mid_up()
                self.two[h][-1].start()
                self.one[h].mid_down()
                self.two[h][1].start()

        def mid(self, e):
            for h in (0, 1):
                self.two[h][e].mid()

        def s4(self):
            for h in (0, 1):
                self.one[h].end()
                self.two[h][2].start()

        def end(self, e):
            for h in (0, 1):
                self.two[h][e].end()

    far = idx(peer, y, z)
    row16 = lax.broadcasted_iota(jnp.int32, (256, 1), 0) & 3

    def project(xx):
        def lhs(q, a=0, b=QW):
            return xg[q, xx, :, :, :, a:b].reshape(256, b - a)

        def dot(l, a, b):
            return lax.dot_general(
                l, wq[:, a:b], (((1,), (1,)), ((), ())), preferred_element_type=F32
            )

        m = MAIN
        main = dot(lhs(0), 0, QW)
        for q in (1, 2, 3):
            main = main + dot(lhs(q), q * QW, (q + 1) * QW)
        tails = (
            dot(lhs(0), m, m + 1536) + dot(lhs(1, 0, 512), m + 1536, m + 2048),
            dot(lhs(1, 512, 1536), m, m + 1024) + dot(lhs(2, 0, 1024), m + 1024, m + 2048),
            dot(lhs(2, 1024, 1536), m, m + 512) + dot(lhs(3), m + 512, m + 2048),
        )
        add = jnp.zeros_like(main)
        for s in range(3):
            qacc[:, 0:320] = tails[s]
            add = jnp.where(row16 == s, pltpu.roll(qacc[...], 256 - (3 - s), 0)[:, 0:320], add)
        qacc[:, 0:320] = main + add
        qacc[:, 320:384] = jnp.zeros((256, 64), F32)
        flat = qacc[...]
        odd = lax.rem(t, 2) == 1
        full = jnp.where(odd, pltpu.roll(flat, 320, 1)[:, 0:256], flat[:, 0:256])
        part = jnp.where(odd, flat[:, 0:128], flat[:, 256:384])
        lane = lax.broadcasted_iota(jnp.int32, (256, 128), 1)
        left = jnp.where(
            lane < 64, pltpu.roll(part, 3, 0), pltpu.roll(pltpu.roll(part, 2, 0), 64, 1)
        )
        right = pltpu.roll(part, 1, 0)
        both = jnp.where(row16 == 3, jnp.concatenate([left, right], axis=1), full)
        qout[pl.ds(xx * 16, 16)] = both.reshape(16, 16, 256).astype(BF16)

    def a2a(src, dst, which, to):
        return pltpu.make_async_remote_copy(
            src_ref=src, dst_ref=dst.at[t],
            send_sem=as_sem.at[which], recv_sem=ar_sem.at[which],
            device_id=(g, to), device_id_type=MESH,
        )

    def a2a_wait(src, dst, which):
        all_of = pltpu.make_async_remote_copy(
            src_ref=src.at[pl.ds(0, N_T - 1)], dst_ref=dst.at[pl.ds(0, N_T - 1)],
            send_sem=as_sem.at[which], recv_sem=ar_sem.at[which],
            device_id=(g, far), device_id_type=MESH,
        )
        all_of.wait_recv()
        sent.append(all_of)

    near_set, far_set = GatherSet(own, 0), GatherSet(peer, 1)

    def across(e):
        got = []
        for h in (0, 1):
            near_set.two[h][e].end()
            ref = xg.at[(pl.ds(2 * h, 2), *line(h, own, e), slice(None), pl.ds(QW - LG, LG))]
            got.append(send(ref, ref, 242 + 2 * OFFS.index(e) + h, far))
        return got

    near_set.s1()
    mine = xg.at[:, xh, y, z, :, 0 : QW - LG]
    over = [send(mine, mine, 160, far)]
    near_set.s2()
    near_set.mid(0)
    near_set.s4()
    over[0].wait_recv()
    far_set.s1()
    near_set.mid(-1)
    near_set.mid(1)
    over += across(0)
    far_set.s2()
    near_set.mid(2)
    for e in (-1, 1, 2):
        over += across(e)
    far_set.mid(0)
    far_set.s4()
    far_set.mid(-1)
    far_set.mid(1)
    loads[0].wait()
    project(own)

    def send_near(i, c):
        to = own * 16 + lax.rem(t + i, 16)
        a2a(qout.at[to], qin, 0, to).start()
        return c

    lax.fori_loop(1, 16, send_near, 0)
    qin[t] = qout[t]
    far_set.mid(2)
    for e in OFFS:
        far_set.end(e)
    for c in over[1:]:
        c.wait_recv()
    project(peer)

    def send_far(i, c):
        to = peer * 16 + lax.rem(t + i, 16)
        a2a(qout.at[to], qin, 0, to).start()
        return c

    lax.fori_loop(0, 16, send_far, 0)

    used = [(lens[0, j] + 127) // 128 for j in range(4)]
    first = [0, used[0], used[0] + used[1], used[0] + used[1] + used[2]]

    def of_group(values, gg):
        total = jnp.int32(0)
        for j in range(4):
            total = total + jnp.where(mig[0, j] == gg, values[j], 0)
        return total

    row_len = [of_group([lens[0, j] for j in range(4)], gg) for gg in range(N_G)]
    pages = [
        [order[0, jnp.clip(of_group(first, gg) + b, 0, 11)] for b in range(4)]
        for gg in range(N_G)
    ]

    def by_row(rows, values):
        kind = (rows & 15) >> 2
        got = jnp.where(kind == 0, values[0], values[1])
        got = jnp.where(kind == 2, values[2], got)
        return jnp.where(kind == 3, values[3], got)

    r16 = lax.broadcasted_iota(jnp.int32, (16, 128), 0)
    angle = (by_row(r16, row_len) + (r16 & 3)).astype(F32) * inv[...]
    lane16 = lax.broadcasted_iota(jnp.int32, (16, 128), 1)
    cosine = jnp.cos(angle)
    sine = jnp.where(lane16 < 64, -jnp.sin(angle), jnp.sin(angle))

    a2a_wait(qout, qin, 0)

    def unpack(block):
        one, two = block[:, 0:128], block[:, 128:256]
        step = r16 & 3
        half = jnp.where(
            step == 0, pltpu.roll(one, 13, 0), pltpu.roll(pltpu.roll(one, 14, 0), 64, 1)
        )
        return one, two, jnp.where(step == 2, pltpu.roll(two, 15, 0), half)

    def pair(p, c):
        e0, e1, low = unpack(qin[2 * p].astype(F32))
        o0, o1, high = unpack(qin[2 * p + 1].astype(F32))
        five = (e0, e1, jnp.where(lane16 < 64, low, pltpu.roll(high, 64, 1)), o0, o1)
        for i, h in enumerate(five):
            turned = h * cosine + pltpu.roll(h, 64, 1) * sine
            heads[5 * p + i] = jnp.where(5 * p + i < 72, turned, h).astype(BF16)
        return c

    lax.fori_loop(0, 16, pair, 0)

    loads[1].wait()
    r128 = lax.broadcasted_iota(jnp.int32, (128, 128), 0)
    c128 = lax.broadcasted_iota(jnp.int32, (128, 128), 1)
    r512 = lax.broadcasted_iota(jnp.int32, (128, 512), 0)
    c512 = lax.broadcasted_iota(jnp.int32, (128, 512), 1)
    lim = by_row(lax.broadcasted_iota(jnp.int32, (128, 1), 0), row_len)
    fresh = (
        (c128 < 16) & ((c128 >> 2) == ((r128 & 15) >> 2)) & ((c128 & 3) <= (r128 & 3))
    )
    pad = jnp.zeros((112, 128), BF16)

    def attend(i, c):
        k = lax.rem(i + 4 * peer, 8)
        queries = heads[pl.ds(8 * k, 8)].reshape(128, 128)

        def scores(keys):
            return lax.dot_general(
                queries, keys, (((1,), (1,)), ((), ())), preferred_element_type=F32
            )

        def page(gg, b, what):
            return kv[pages[gg][b], what, k]

        cached = [
            scores(jnp.concatenate([page(gg, b, 0) for b in range(4)], axis=0))
            for gg in range(N_G)
        ]
        cached = by_row(r512, cached) * SCALE
        live = c512 < lim
        cached = jnp.where(live, cached, NEG_FILL)
        newest = scores(jnp.concatenate([heads[64 + k], pad], axis=0)) * SCALE
        newest = jnp.where(fresh, newest, NEG_FILL)
        top = jnp.maximum(
            jnp.max(cached, axis=-1, keepdims=True), jnp.max(newest, axis=-1, keepdims=True)
        )
        weights = jnp.where(live, jnp.exp(cached - top), 0.0).astype(BF16)
        extra = jnp.where(fresh, jnp.exp(newest - top), 0.0).astype(BF16)
        total = jnp.sum(weights.astype(F32), axis=-1, keepdims=True) + jnp.sum(
            extra.astype(F32), axis=-1, keepdims=True
        )
        acc = []
        for pair_of in ((0, 1), (2, 3)):
            values = jnp.concatenate(
                [
                    jnp.concatenate([page(gg, b, 1) for b in range(4)], axis=0)
                    for gg in pair_of
                ],
                axis=1,
            )
            two = jnp.dot(weights, values, preferred_element_type=F32)
            acc += [two[:, 0:128], two[:, 128:256]]
        acc = by_row(r128, acc) + jnp.dot(
            extra,
            jnp.concatenate([heads[72 + k], pad], axis=0),
            preferred_element_type=F32,
        )
        att[pl.ds(4 * k, 4)] = (acc / total).reshape(4, 2, 16, 128).astype(BF16)

        def give(i, c):
            to = 4 * k + i

            @pl.when(to != t)
            def _():
                a2a(att.at[to], ain, 1, to).start()

            return c

        lax.fori_loop(0, 4, give, 0)
        return c

    lax.fori_loop(0, 8, attend, 0, unroll=2)
    ain[t] = att[t]
    loads[2].wait()
    a2a_wait(att, ain, 1)

    def lhs_of(xx):
        left = jnp.concatenate(
            [ain[pl.ds(xx * 16, 16), i].reshape(256, 128) for i in (0, 1)], axis=1
        )
        wide = left.astype(F32)
        return left, [pltpu.roll(wide, 3 - s, 0).astype(BF16) for s in range(3)]

    def expand(sides, xx, q):
        left, turned = sides
        for c in range(3 * q, 3 * q + 3):
            at = MAIN + (c % 4) * CHUNK
            main = jnp.dot(
                left, wo[:, c * CHUNK : (c + 1) * CHUNK], preferred_element_type=F32
            )
            tail = jnp.dot(turned[c // 4], wo[:, at : at + CHUNK], preferred_element_type=F32)
            lane = (c % 3) * CHUNK
            terms[c // 3, xx, :, :, :, lane : lane + CHUNK] = (
                jnp.where(row16 == 3, tail, main).reshape(4, 4, 16, CHUNK).astype(BF16)
            )

    class Reduce:
        def __init__(self, at, q, k, n, lanes):
            self.at, self.to = at
            self.q, self.k, self.n = q, k, n
            self.lanes = slice(0, lanes)

        def part(self, o, i):
            return (self.q + i, *self.at(o), slice(None), self.lanes)

        def both(self, o):
            return (pl.ds(self.q, 2), *self.at(o), slice(None), self.lanes)

        def s1(self, i):
            k, n, w = self.k, self.n, self.lanes
            if i == 0:
                self.up = send(terms.at[self.part(2, 0)], rq.at[n, 0, :, w], k, self.to(1))
            else:
                self.down = send(
                    terms.at[self.part(-2, 1)], rq.at[n, 1, :, w], k + 1, self.to(-1)
                )

        def s2(self):
            k, n, w = self.k, self.n, self.lanes
            for i, d, came in ((0, 1, self.up), (1, -1, self.down)):
                came.wait_recv()
                p = self.part(d, i)
                terms[p] = (terms[p].astype(F32) + rq[n, i, :, w].astype(F32)).astype(BF16)
                on = send(
                    terms.at[self.both(d)], rf.at[n, i, :, :, w], k + 2 + i, self.to(d)
                )
                if i == 0:
                    self.up2 = on
                else:
                    self.down2 = on

        def s3(self):
            n, w = self.n, self.lanes
            self.up2.wait_recv()
            self.down2.wait_recv()
            for i in (0, 1):
                p = self.part(0, i)
                terms[p] = (
                    terms[p].astype(F32)
                    + rf[n, 0, i, :, w].astype(F32)
                    + rf[n, 1, i, :, w].astype(F32)
                ).astype(BF16)

    class ReduceSet:
        def __init__(self, xx, n):
            k, m = 161 + 40 * n, 10 * n
            lanes = QW - LR if n == 0 else QW
            self.big = [
                {
                    e: Reduce(
                        ring_second(h, xx, e), 2 * h, k + 20 * h + 4 * i, m + 5 * h + i, lanes
                    )
                    for i, e in enumerate(OFFS)
                }
                for h in (0, 1)
            ]
            self.last = [
                Reduce(ring_first(h, xx), 2 * h, k + 20 * h + 16, m + 5 * h + 4, lanes)
                for h in (0, 1)
            ]

        def s1(self, h, i, *es):
            for e in es:
                self.big[h][e].s1(i)

        def s2(self, *es):
            for e in es:
                for h in (0, 1):
                    self.big[h][e].s2()

        def s3(self, *es):
            for e in es:
                for h in (0, 1):
                    self.big[h][e].s3()

        def l1(self):
            for h in (0, 1):
                self.last[h].s1(0)
                self.last[h].s1(1)

        def l2(self):
            for h in (0, 1):
                self.last[h].s2()

        def l3(self):
            for h in (0, 1):
                self.last[h].s3()

    far_sum, near_sum = ReduceSet(peer, 0), ReduceSet(own, 1)
    BACK = (2, -1, 1, 0)
    cross = {}

    def hand(h):
        for i, e in enumerate(BACK):
            lanes = pl.ds(QW - LR, LR)
            _, yy, zz = line(h, peer, e)
            cross[h, e] = send(
                terms.at[pl.ds(2 * h, 2), peer, yy, zz, :, lanes],
                rc.at[pl.ds(2 * h, 2), yy, zz],
                250 + 4 * h + i,
                far,
            )

    def take(h, e):
        cross[h, e].wait_recv()
        for q in (2 * h, 2 * h + 1):
            for o in range(4):
                _, yy, zz = place(spot, h, own, e, o)
                old = terms[q, own, yy, zz, :, QW - LR : QW].astype(F32)
                terms[q, own, yy, zz, :, QW - LR : QW] = (
                    old + rc[q, yy, zz].astype(F32)
                ).astype(BF16)
        near_sum.s1(h, 0, e)
        near_sum.s1(h, 1, e)

    sides = lhs_of(peer)
    for q in (0, 2, 1, 3):
        expand(sides, peer, q)
        far_sum.s1(q // 2, q % 2, *BACK)
    hand(0)
    hand(1)
    far_sum.s2(*BACK)
    sides = lhs_of(own)
    for q in range(4):
        expand(sides, own, q)
    take(0, 2)
    take(1, 2)
    far_sum.s3(2)
    far_sum.l1()
    take(0, -1)
    take(1, -1)
    near_sum.s2(2)
    far_sum.s3(-1, 1)
    far_sum.l2()
    take(0, 1)
    take(1, 1)
    near_sum.s2(-1)
    far_sum.s3(0)
    far_sum.l3()
    over = send(terms.at[:, peer, y, z, :, 0 : QW - LR], rx, 241, far)
    take(0, 0)
    take(1, 0)
    near_sum.s2(1)
    near_sum.s3(2)
    near_sum.l1()
    near_sum.s2(0)
    near_sum.s3(-1, 1)
    near_sum.l2()
    near_sum.s3(0)
    near_sum.l3()
    over.wait_recv()
    for q in range(4):
        x32[q, :, 0 : QW - LR] = terms[q, xh, y, z, :, 0 : QW - LR].astype(F32) + rx[q].astype(F32)
        x32[q, :, QW - LR : QW] = terms[q, xh, y, z, :, QW - LR : QW].astype(F32)
    for gg in range(N_G):
        for q in range(4):
            stage[gg, 4 * q : 4 * q + 4, :] = x32[q, 4 * gg : 4 * gg + 4, :]
    for gg in range(N_G):
        fsend[gg] = stage[gg].astype(BF16)
    sent.extend(group_exchange(fsend, frecv, N_G))
    for s in range(N_G):
        stage[s] = frecv[s].astype(F32)
        for j in range(3):
            for q in range(4):
                o32[j, s : s + 1, q * QW : (q + 1) * QW] = stage[
                    s, 4 * q + j : 4 * q + j + 1, :
                ]
            for c in range(4 * j, 4 * j + 4):
                at = MAIN + (c % 4) * CHUNK
                lane = (c % 3) * CHUNK
                row = 4 * (c // 3) + 3
                o32[j, s : s + 1, at : at + CHUNK] = stage[
                    s, row : row + 1, lane : lane + CHUNK
                ]
    for j in range(3):
        out[j] = o32[j].astype(BF16)
    for c in sent:
        c.wait_send()


def per_device(tokens, norm_gain, w_qkv, w_out, lengths, migrate, page_order, kv_pool):
    inverse = np.float32(ROPE_BASE) ** (-(np.arange(64, dtype=np.float32) * np.float32(2.0) / 128))
    inverse = jnp.asarray(np.concatenate([inverse, inverse]).reshape(1, 128), F32)
    vmem = pl.BlockSpec(memory_space=pltpu.VMEM)
    hbm = pl.BlockSpec(memory_space=pl.ANY)
    dma = pltpu.SemaphoreType.DMA
    done = pl.pallas_call(
        body,
        out_shape=jax.ShapeDtypeStruct((3, 4, D), BF16),
        in_specs=[hbm] * 9,
        out_specs=vmem,
        scratch_shapes=[
            pltpu.VMEM((1, D), F32),
            pltpu.VMEM((1, 128), F32),
            pltpu.SMEM((1, 4), jnp.int32),
            pltpu.SMEM((1, 4), jnp.int32),
            pltpu.SMEM((1, 12), jnp.int32),
            pltpu.VMEM((3, 4, D), BF16),
            pltpu.VMEM((4, 16, QW), F32),
            pltpu.VMEM((4, 16, QW), BF16),
            pltpu.VMEM((4, 16, QW), BF16),
            pltpu.VMEM((4, 16, QW), F32),
            pltpu.VMEM((4, 2, 4, 4, 16, QW), BF16),
            pltpu.VMEM((320, D), BF16),
            pltpu.VMEM((256, D), BF16),
            pltpu.VMEM((12, 2, 8, 128, 128), BF16),
            pltpu.VMEM((256, 384), F32),
            pltpu.VMEM((32, 16, 256), BF16),
            pltpu.VMEM((32, 16, 256), BF16),
            pltpu.VMEM((80, 16, 128), BF16),
            pltpu.VMEM((32, 2, 16, 128), BF16),
            pltpu.VMEM((32, 2, 16, 128), BF16),
            pltpu.VMEM((4, 2, 4, 4, 16, QW), BF16),
            pltpu.VMEM((20, 2, 16, QW), BF16),
            pltpu.VMEM((20, 2, 2, 16, QW), BF16),
            pltpu.VMEM((4, 16, QW - LR), BF16),
            pltpu.VMEM((4, 4, 4, 16, LR), BF16),
            pltpu.VMEM((4, 16, QW), BF16),
            pltpu.VMEM((4, 16, QW), BF16),
            pltpu.VMEM((3, 4, D), F32),
            dma((9,)),
            dma((2 * N_G,)),
            dma((2 * N_G,)),
            dma((258,)),
            dma((258,)),
            dma((2,)),
            dma((2,)),
        ],
        compiler_params=pltpu.CompilerParams(
            collective_id=0, has_side_effects=True, vmem_limit_bytes=60 * 2**20
        ),
        cost_estimate=pl.CostEstimate(
            flops=4 * 10**9, bytes_accessed=17 * 10**6, transcendentals=10**6
        ),
    )(
        norm_gain.reshape(1, D), inverse, lengths, migrate, page_order,
        tokens.transpose(1, 0, 2), w_qkv.T, w_out, kv_pool.reshape(12, 2, 8, 128, 128),
    )
    return (tokens.astype(F32) + done.transpose(1, 0, 2).astype(F32)).astype(BF16)


def solution(mesh):
    both = ("group", "tensor")
    return jax.shard_map(
        per_device,
        mesh=mesh,
        in_specs=(
            P(both, None, None),
            P(),
            P(None, "tensor"),
            P("tensor", None),
            P(both, None),
            P(both, None),
            P(both, None),
            P(both, None, None, None, None, None),
        ),
        out_specs=P(both, None, None),
        check_vma=False,
    )
```
